512 devices in a mesh: vis: 8 (over z), ctx: 32 (over x, y), tp: 2 (over core).
Axes of the slice: x: 4, y: 8, z: 8, core: 2. Of those that a mesh axis runs over, the one named last changes fastest.
Arguments:
- patch_rows: bfloat16 [4096, 1280], P('ctx'), may hold values from -6 to 6
- vit_gain: float32 [1280], replicated, may hold values from 0.25 to 1.75
- vit_bias: float32 [1280], replicated, may hold values from -3 to 3
- vit_qkv: bfloat16 [1280, 3, 16, 80], P(None, None, ('vis', 'tp')), as said below
- vit_out: bfloat16 [16, 80, 1280], P(('vis', 'tp')), may hold values from -0.15625 to 0.15625
- merge_gain: float32 [1280], replicated, may hold values from 0.25 to 1.75
- merge_bias: float32 [1280], replicated, may hold values from -3 to 3
- merge_weight: bfloat16 [5120, 4096], P('ctx', ('vis', 'tp')), may hold values from -0.078125 to 0.078125
- image_patches: int32 [32, 2], replicated, may hold values from 4 to 64, as said below
- window_ids: int32 [4096], P('ctx'), may hold values from 0 to 4095, as said below
- image_pos: int32 [1024], replicated, may hold values from 0 to 4095, as said below
- slice_order: int32 [32], replicated, may hold values from 0 to 31, as said below
- doc_ids: int32 [4096], replicated, may hold values from 0 to 15, never falling along the last dimension, each value on 1 to 512 neighbouring positions
- text_rows: bfloat16 [4096, 4096], P('ctx', ('vis', 'tp')), may hold values from -6 to 6
- norm_gain: float32 [4096], replicated, may hold values from 0.25 to 1.75
- w_query: bfloat16 [4096, 8, 4, 128], P(None, 'vis', 'tp'), as said below
- w_keyval: bfloat16 [2, 4096, 8, 128], P('tp', None, 'vis'), as said below
Outputs:
- attention_out: bfloat16 [4096, 8, 512], P('ctx', 'vis', 'tp')
The draws below stay inside these ranges and needn't reach their ends.
Inputs may be any that keep to these rules, and one draw needn't show every extreme that they name: `image_patches`: each is h * w for an image of h by w patches, h and w even and at most 32; the images of one ctx shard hold at most 128 patches together, exactly 128 on some shard. `window_ids`: equal ids mark one attention window: consecutive slots of one ctx shard, a multiple of 4 of them and at most 64, never in two images; slots after a shard's live patches form windows of 4. `slice_order`: a permutation; ctx shard c holds the sequence slices slice_order[c] and 63 - slice_order[c] of 64 positions, in that order, as its 128 rows. `image_pos`: distinct positions, one for every merged slot, live or not; the 32 slots of any one ctx shard put exactly 1 positions into the rows of each ctx shard. `doc_ids`: never falling along positions; each document holds 1 to 512 positions. `vit_qkv`: independent centred entries. `w_query`: independent centred entries. `w_keyval`: independent centred entries.
All inputs are finite; a program needn't handle non-finite values.
Results may differ from the reference program's by a relative error of at most 0.022.
The reference program's roundings to bfloat16 on the way count: a program that leaves them out, or rounds other values in their place, can miss the bound.
Values may be sent and summed in bfloat16 or wider, within the bound.
A program may use at most 64 MiB of HBM per device.

```python
import math
import jax
import jax.numpy as jnp
import numpy as np
from jax import lax

D = 4096
HD = 128
KVH = 8
QPG = 4
VD = 1280
VH = 16
VHD = 80
IMGS = 2
TOK = 128
PCAP = 128
SHARDS = 32
SEQ = 4096
HALF = 64
ICAP = 32
IMGMAX = 64
DOCS = 16
DOCMAX = 512


def image_grids(seed_key):
    base_key = jax.random.fold_in(seed_key, 101)
    height_key, width_key, full_key = jax.random.split(base_key, 3)
    heights = 2 * jax.random.randint(height_key, (SHARDS, IMGS), 1, 17)
    width_cap = jnp.minimum(32, IMGMAX // heights // 2 * 2)
    widths = 2 * jax.random.randint(width_key, (SHARDS, IMGS), 1, width_cap // 2 + 1)
    full_shard = jax.random.randint(full_key, (), 0, SHARDS)
    if IMGMAX <= 64:
        full_height = 8
    elif IMGMAX <= 256:
        full_height = 16
    else:
        full_height = 32
    is_full = (jnp.arange(SHARDS) == full_shard)[:, None]
    heights = jnp.where(is_full, full_height, heights)
    widths = jnp.where(is_full, IMGMAX // full_height, widths)
    return (heights.astype(jnp.int32), widths.astype(jnp.int32))


def draw_image_patches(key, part):
    heights, widths = image_grids(key)
    return (heights * widths).astype(jnp.int32)


def draw_window_ids(key, part):
    heights, widths = image_grids(key)
    corner = 8 * jnp.arange(4, dtype=jnp.int32)
    tall = jnp.clip(heights[:, :, None] - corner, 0, 8)
    broad = jnp.clip(widths[:, :, None] - corner, 0, 8)
    sizes = (tall[:, :, :, None] * broad[:, :, None, :]).reshape(SHARDS, IMGS * 16)
    ends = jnp.cumsum(sizes, axis=1)
    slot_ids = jnp.arange(PCAP, dtype=jnp.int32)
    inside = jnp.sum((ends[:, None, :] <= slot_ids[None, :, None]).astype(jnp.int32), axis=2)
    filled = ends[:, -1:]
    spare = IMGS * 16 + (slot_ids[None, :] - filled) // 4
    local_ids = jnp.where(slot_ids[None, :] >= filled, spare, inside)
    return (local_ids + jnp.arange(SHARDS, dtype=jnp.int32)[:, None] * PCAP).reshape(SHARDS * PCAP).astype(jnp.int32)


def shuffle_rows(seed_key):
    return jax.random.permutation(seed_key, TOK).astype(jnp.int32)


def shard_layout(seed_key):
    base_key = jax.random.fold_in(seed_key, 202)
    slice_key, order_key, row_key = jax.random.split(base_key, 3)
    slice_order = jax.random.permutation(slice_key, SHARDS).astype(jnp.int32)
    dest_order = jax.random.permutation(order_key, SHARDS).astype(jnp.int32)
    row_orders = jax.vmap(shuffle_rows)(jax.random.split(row_key, SHARDS))
    send_each = ICAP // SHARDS
    source = jnp.arange(SHARDS, dtype=jnp.int32)[:, None]
    slot_ids = jnp.arange(ICAP, dtype=jnp.int32)[None, :]
    target = dest_order[(source + slot_ids // send_each) % SHARDS]
    entry = source * send_each + slot_ids % send_each
    rows_at = row_orders[target, entry]
    slices = jnp.where(rows_at < HALF, slice_order[target], 2 * SHARDS - 1 - slice_order[target])
    positions = slices * HALF + rows_at % HALF
    return (slice_order, positions.reshape(SHARDS * ICAP).astype(jnp.int32))


def draw_slice_order(key, part):
    slice_order, positions = shard_layout(key)
    return slice_order


def draw_image_pos(key, part):
    slice_order, positions = shard_layout(key)
    return positions


def draw_vit_qkv(key, part):
    noise = jax.random.normal(jax.random.fold_in(key, 303), (VD, 3, VH, VHD), jnp.float32)
    return (noise * (1.0 / math.sqrt(VD))).astype(jnp.bfloat16)


def draw_w_query(key, part):
    noise = jax.random.normal(jax.random.fold_in(key, 404), (D, KVH, QPG, HD), jnp.float32)
    boost = 1.0
    return (noise * (boost / math.sqrt(D))).astype(jnp.bfloat16)


def draw_w_keyval(key, part):
    noise = jax.random.normal(jax.random.fold_in(key, 505), (2, D, KVH, HD), jnp.float32)
    return (noise * (1.0 / math.sqrt(D))).astype(jnp.bfloat16)


def block_scale(rng, shape, cuts, low, high):
    level = 1.0
    for position, blocks in cuts:
        steps = jax.random.uniform(jax.random.fold_in(jax.random.fold_in(rng, 6), position), (blocks,), jnp.float32, low / len(cuts), high / len(cuts))
        level = level * jnp.repeat(jnp.exp(steps), shape[position] // blocks).reshape((-1,) + (1,) * (len(shape) - 1 - position))
    return level


def profile(amount, total, most, skew):
    loads = [(1 << 20) // math.isqrt(grade ** skew) + 1 for grade in range(2, amount + 1)]
    surplus, holding = total - most - (amount - 1), [1] * (amount - 1)
    while surplus > 0:
        movable = [i for i in range(amount - 1) if holding[i] < most]
        whole, left = sum([loads[i] for i in movable]), surplus
        for i in movable:
            more = min(most - holding[i], max(1, left * loads[i] // whole), surplus)
            holding[i] = holding[i] + more
            surplus = surplus - more
    return np.array([most] + holding)


def uneven_parts(stream_key, amount, total, reach, slope):
    if amount == 2:
        one = jax.random.randint(stream_key, (), max(1, total - reach), min(reach, total - 1) + 1)
        return jnp.stack([one, total - one])
    sizes = jnp.asarray(profile(amount, total, reach, slope), jnp.int32)
    pairs = (amount - 1) // 2
    donor, receiver = sizes[1:1 + 2 * pairs:2], sizes[2:2 + 2 * pairs:2]
    room = jnp.minimum(donor - 1, reach - receiver)
    shifted = jax.random.randint(jax.random.fold_in(stream_key, 1), (pairs,), 0, 1 << 20) % (room + 1)
    sizes = sizes.at[1:1 + 2 * pairs:2].set(donor - shifted).at[2:2 + 2 * pairs:2].set(receiver + shifted)
    return sizes[jax.random.permutation(jax.random.fold_in(stream_key, 2), amount)]


def scatter_about(rng, dims, width, most, pieces=(), held_as=jnp.bfloat16):
    result = jax.random.normal(rng, dims, jnp.float32) * width
    if len(pieces) > 0:
        result = block_scale(rng, dims, pieces, -0.22, 0.18) * result
    return jnp.clip(result, min=-most, max=most).astype(held_as)


def setup_inputs(seed: int = 0) -> dict:
    key_list = jax.random.split(jax.random.key(seed), 18)
    return {
        "patch_rows": scatter_about(key_list[0], (SHARDS * PCAP, VD), 1.0, 6.0, ((0, 32),)),
        "vit_gain": jnp.clip(1.0 + 0.15 * jax.random.normal(key_list[1], (VD,), jnp.float32), 0.25, 1.75),
        "vit_bias": scatter_about(key_list[2], (VD,), 0.5, 3.0, (), jnp.float32),
        "vit_qkv": draw_vit_qkv(jax.random.fold_in(key_list[17], 71), 0),
        "vit_out": scatter_about(key_list[4], (VH, VHD, VD), (VH * VHD) ** -0.5, 0.15625, ((0, 16),)),
        "merge_gain": jnp.clip(1.0 + 0.15 * jax.random.normal(key_list[5], (VD,), jnp.float32), 0.25, 1.75),
        "merge_bias": scatter_about(key_list[6], (VD,), 0.5, 3.0, (), jnp.float32),
        "merge_weight": scatter_about(key_list[7], (4 * VD, D), (4 * VD) ** -0.5, 0.078125, ((0, 32), (1, 16))),
        "image_patches": draw_image_patches(jax.random.fold_in(key_list[17], 71), 0),
        "window_ids": draw_window_ids(jax.random.fold_in(key_list[17], 71), 0),
        "image_pos": draw_image_pos(jax.random.fold_in(key_list[17], 71), 0),
        "slice_order": draw_slice_order(jax.random.fold_in(key_list[17], 71), 0),
        "doc_ids": jnp.searchsorted(jnp.cumsum(uneven_parts(key_list[12], DOCS, SEQ, DOCMAX, 0)), jnp.arange(SEQ), side="right").astype(jnp.int32),
        "text_rows": scatter_about(key_list[13], (SEQ, D), 1.0, 6.0, ((0, 32), (1, 16))),
        "norm_gain": jnp.clip(1.0 + 0.15 * jax.random.normal(key_list[14], (D,), jnp.float32), 0.25, 1.75),
        "w_query": draw_w_query(jax.random.fold_in(key_list[17], 71), 0),
        "w_keyval": draw_w_keyval(jax.random.fold_in(key_list[17], 71), 0),
    }


norm_eps = 1e-06
rope_base = 1000000.0
big_negative = -1e+30

def layer_norm(values, scale_vec, shift_vec):
    centre = lax.optimization_barrier(jnp.mean(values, axis=-1, keepdims=True))
    offset = values - centre
    spread = lax.optimization_barrier(jnp.mean(offset * offset, axis=-1, keepdims=True))
    return offset * lax.rsqrt(spread + norm_eps) * scale_vec + shift_vec

def rotate(values, positions):
    half_dim = values.shape[-1] // 2
    exponent = jnp.arange(half_dim, dtype=jnp.float32) * (-2.0 / values.shape[-1])
    frequency = jnp.power(jnp.float32(rope_base), exponent)
    angles = positions.astype(jnp.float32)[:, None] * frequency[None, :]
    shape_out = (values.shape[0],) + (1,) * (values.ndim - 2) + (half_dim,)
    cosine = jnp.cos(angles).reshape(shape_out)
    sine_part = jnp.sin(angles).reshape(shape_out)
    lead_half = values[..., :half_dim]
    tail_half = values[..., half_dim:]
    return jnp.concatenate([lead_half * cosine - tail_half * sine_part, tail_half * cosine + lead_half * sine_part], axis=-1)

def row_positions(row_ids, slice_order, tokens_dev):
    shards = slice_order.shape[0]
    device_of = row_ids // tokens_dev
    local_row = row_ids % tokens_dev
    half_tok = tokens_dev // 2
    matches = device_of[:, None] == jnp.arange(shards, dtype=jnp.int32)[None, :]
    first_slice = lax.optimization_barrier(jnp.sum(jnp.where(matches, slice_order[None, :], 0), axis=1)).astype(jnp.int32)
    slice_ids = jnp.where(local_row < half_tok, first_slice, 2 * shards - 1 - first_slice)
    return (slice_ids * half_tok + local_row % half_tok).astype(jnp.int32)

def place_of(positions, slice_order, tokens_dev):
    shards = slice_order.shape[0]
    half_tok = tokens_dev // 2
    slice_ids = positions // half_tok
    paired = jnp.minimum(slice_ids, 2 * shards - 1 - slice_ids)
    owner_hot = (paired[..., None] == slice_order).astype(jnp.int32)
    owner_dev = lax.optimization_barrier(jnp.sum(owner_hot * jnp.arange(shards, dtype=jnp.int32), axis=-1)).astype(jnp.int32)
    local_row = (jnp.where(slice_ids < shards, 0, half_tok) + positions % half_tok).astype(jnp.int32)
    return (owner_dev, local_row, owner_hot)

def vision_block(patch_block, window_block, vit_gain, vit_bias, vit_qkv, vit_out, merge_gain, merge_bias):
    vit_width = vit_qkv.shape[0]
    vit_heads = vit_qkv.shape[2]
    head_dim = vit_qkv.shape[3]
    slot_count = patch_block.shape[0]
    normed = layer_norm(patch_block.astype(jnp.float32), vit_gain, vit_bias).astype(jnp.bfloat16)
    projected = jnp.dot(normed, vit_qkv.reshape(vit_width, 3 * vit_heads * head_dim), preferred_element_type=jnp.float32)
    projected = lax.optimization_barrier(projected.astype(jnp.bfloat16)).astype(jnp.float32)
    projected = projected.reshape(slot_count, 3, vit_heads, head_dim)
    scores = jnp.einsum('qhd,khd->hqk', projected[:, 0], projected[:, 1]) / math.sqrt(head_dim)
    allowed = window_block[:, None] == window_block[None, :]
    scores = jnp.where(allowed[None], scores, big_negative)
    powers = jnp.exp(scores - lax.optimization_barrier(jnp.max(scores, axis=-1, keepdims=True)))
    totals = lax.optimization_barrier(jnp.sum(powers, axis=-1))
    rounded = lax.optimization_barrier(powers.astype(jnp.bfloat16)).astype(jnp.float32)
    blended = jnp.einsum('hqk,khd->qhd', rounded, projected[:, 2]) / jnp.transpose(totals)[:, :, None]
    blended = blended.astype(jnp.bfloat16).reshape(slot_count, vit_heads * head_dim)
    branch_sum = jnp.dot(blended, vit_out.reshape(vit_heads * head_dim, vit_width), preferred_element_type=jnp.float32)
    hidden = patch_block.astype(jnp.float32) + branch_sum
    merged = layer_norm(hidden, merge_gain, merge_bias).astype(jnp.bfloat16)
    return merged.reshape(slot_count // 4, 4 * vit_width)

def reference(patch_rows, vit_gain, vit_bias, vit_qkv, vit_out, merge_gain, merge_bias, merge_weight, image_patches, window_ids, image_pos, slice_order, doc_ids, text_rows, norm_gain, w_query, w_keyval):

    def one_shard(inputs_now):
        patch_block, window_block = inputs_now
        return vision_block(patch_block, window_block, vit_gain, vit_bias, vit_qkv, vit_out, merge_gain, merge_bias)
    merged = lax.map(one_shard, (patch_rows.reshape(SHARDS, PCAP, VD), window_ids.reshape(SHARDS, PCAP)))
    image_emb = jnp.dot(merged.reshape(SHARDS * ICAP, 4 * VD), merge_weight, preferred_element_type=jnp.float32).astype(jnp.bfloat16)
    live_count = (lax.optimization_barrier(jnp.sum(image_patches, axis=1)) // 4).astype(jnp.int32)
    slot_ids = jnp.arange(ICAP, dtype=jnp.int32)
    is_live = (slot_ids[None, :] < live_count[:, None]).reshape(SHARDS * ICAP)
    owner_dev, local_row, owner_hot = place_of(image_pos, slice_order, TOK)
    target = jnp.where(is_live, owner_dev * TOK + local_row, SEQ).astype(jnp.int32)
    embeds = text_rows.at[target].set(image_emb, mode='drop')
    widened = embeds.astype(jnp.float32)
    normed = (widened * lax.rsqrt(lax.optimization_barrier(jnp.mean(widened * widened, axis=1, keepdims=True)) + norm_eps) * norm_gain).astype(jnp.bfloat16)
    positions = row_positions(jnp.arange(SEQ, dtype=jnp.int32), slice_order, TOK)
    doc_of = jnp.take(doc_ids, positions)
    queries = jnp.dot(normed, w_query.reshape(D, KVH * QPG * HD), preferred_element_type=jnp.float32).reshape(SEQ, KVH, QPG, HD)
    queries = rotate(queries, positions).astype(jnp.bfloat16)
    keys_all = jnp.dot(normed, w_keyval[0].reshape(D, KVH * HD), preferred_element_type=jnp.float32).reshape(SEQ, KVH, HD)
    keys_all = rotate(keys_all, positions).astype(jnp.bfloat16)
    values_all = jnp.dot(normed, w_keyval[1].reshape(D, KVH * HD), preferred_element_type=jnp.float32).astype(jnp.bfloat16).reshape(SEQ, KVH, HD)
    keys_heads = jnp.transpose(keys_all, (1, 0, 2)).astype(jnp.float32)
    values_heads = jnp.transpose(values_all, (1, 0, 2)).astype(jnp.float32)
    query_block = math.gcd(SEQ, 512)

    def one_block(block_index):
        first_row = block_index * query_block
        query_rows = lax.dynamic_slice_in_dim(queries, first_row, query_block, 0).astype(jnp.float32)
        query_pos = lax.dynamic_slice_in_dim(positions, first_row, query_block, 0)
        query_doc = lax.dynamic_slice_in_dim(doc_of, first_row, query_block, 0)
        allowed = (positions[None, :] <= query_pos[:, None]) & (doc_of[None, :] == query_doc[:, None])

        def one_head(inputs_now):
            head_queries, head_keys, head_values = inputs_now
            scores = jnp.einsum('qgd,kd->gqk', head_queries, head_keys) / math.sqrt(HD)
            scores = jnp.where(allowed[None], scores, big_negative)
            powers = jnp.exp(scores - lax.optimization_barrier(jnp.max(scores, axis=-1, keepdims=True)))
            totals = lax.optimization_barrier(jnp.sum(powers, axis=-1))
            rounded = lax.optimization_barrier(powers.astype(jnp.bfloat16)).astype(jnp.float32)
            blended = jnp.einsum('gqk,kd->qgd', rounded, head_values) / jnp.transpose(totals)[:, :, None]
            return blended.astype(jnp.bfloat16)
        per_head = lax.map(one_head, (jnp.transpose(query_rows, (1, 0, 2, 3)), keys_heads, values_heads))
        return jnp.transpose(per_head, (1, 0, 2, 3)).reshape(query_block, KVH, QPG * HD)
    blocks = lax.map(one_block, jnp.arange(SEQ // query_block, dtype=jnp.int32))
    return blocks.reshape(SEQ, KVH, QPG * HD)
```

```python
import functools
import math

import jax
import jax.numpy as jnp
import numpy as np
from jax import lax
from jax.experimental import pallas as pl
from jax.experimental.pallas import tpu as pltpu
from jax.sharding import PartitionSpec as P

D = 4096
HD = 128
VD = 1280
VHD = 80
TOK = 128
NV, NX, NY, NT = 8, 4, 8, 2
NC = NX * NY

norm_eps = 1e-06
rope_base = 1000000.0
big_negative = -1e30
MESH = pl.DeviceIdType.MESH
F32 = jnp.float32
BF = jnp.bfloat16


def nn(a, b):
    return lax.dot_general(a, b, (((1,), (0,)), ((), ())), preferred_element_type=F32)


def nt(a, b):
    return lax.dot_general(a, b, (((1,), (1,)), ((), ())), preferred_element_type=F32)


def iota(shape, dim):
    return lax.broadcasted_iota(jnp.int32, shape, dim)


def hot(mask):
    return jnp.where(mask, 1.0, 0.0).astype(BF)


def layer_norm(values, scale_vec, shift_vec):
    centre = jnp.mean(values, axis=-1, keepdims=True)
    offset = values - centre
    spread = jnp.mean(offset * offset, axis=-1, keepdims=True)
    return offset * lax.rsqrt(spread + norm_eps) * scale_vec + shift_vec


def rotate(values, cosine, sine):
    return values * cosine + pltpu.roll(values, 64, 1) * sine


def angles_of(pos_column, freq_row):
    ang = pos_column * freq_row
    sign = jnp.where(iota(ang.shape, 1) < 64, -1.0, 1.0)
    return jnp.cos(ang), jnp.sin(ang) * sign


def fold(rows8):
    return jnp.concatenate([rows8[:, :640], rows8[:, 640:]], axis=0)


def unfold(rows16):
    return jnp.concatenate([rows16[:8], rows16[8:]], axis=1)


def kernel(
    patch, vgain, vbias, wqkv, vout, mgain, mbias, wblk, ipatch, wids, ipos, sorder, sorder_v, docs,
    text, ngain, wq_raw, wkv_in, freq, out,
    wq_land, wq, wkv, wbuf, tbuf, ntext, kvbuf, kibuf, blp, mixb, vo, pp, res,
    rs_src, rs_buf, ag, ysrc, ybuf, p4, nimg, qsrc, qbuf, kpos_s,
    lsem, x1s, x1r, vos, vor, ress, resr, ws, wr, ts, tr, rss, rsr, ags, agr, ys, yr,
    p4s, p4r, kvs, kvr, kis, kir, qs, qr, fs, fr,
):
    v, c, t = lax.axis_index("vis"), lax.axis_index("ctx"), lax.axis_index("tp")
    x, y = c // NY, lax.rem(c, NY)
    other = 1 - t

    def at_v(k):
        return (lax.rem(v + k, NV), c, t)

    def at_c(k):
        return (v, lax.rem(c + k, NC), t)

    def at_y(k):
        return (v, x * NY + lax.rem(y + k, NY), t)

    def at_x(k, tt):
        return (v, lax.rem(x + k, NX) * NY + y, tt)

    partner = (v, c, other)

    barrier = pltpu.get_barrier_semaphore()

    def greet(d):
        pl.semaphore_signal(barrier, inc=1, device_id=d, device_id_type=MESH)

    lax.fori_loop(1, NV, lambda k, z: (greet(at_v(k)), z)[1], 0)
    lax.fori_loop(1, NC, lambda k, z: (greet(at_c(k)), z)[1], 0)
    for k in range(1, NX):
        greet(at_x(k, other))
    greet(partner)
    greetings = (NV - 1) + (NC - 1) + (NX - 1) + 1

    loads = [
        pltpu.make_async_copy(wq_raw, wq_land, lsem.at[0]),
        pltpu.make_async_copy(wkv_in, wkv, lsem.at[1]),
        pltpu.make_async_copy(vout, vo.at[t], lsem.at[2]),
        pltpu.make_async_copy(text, tbuf.at[t, v], lsem.at[3]),
        pltpu.make_async_copy(wblk, wbuf.at[y], lsem.at[4]),
    ]
    for load in loads:
        load.start()

    def remote(src, dst, ssem, rsem, d):
        return pltpu.make_async_remote_copy(
            src_ref=src, dst_ref=dst, send_sem=ssem, recv_sem=rsem, device_id=d, device_id_type=MESH
        )

    normed = layer_norm(patch[...].astype(F32), vgain[...], vbias[...]).astype(BF)
    vq = nt(normed, wqkv[0:80, :]).astype(BF)
    vk = nt(normed, wqkv[80:160, :]).astype(BF)
    vv = nt(normed, wqkv[160:240, :]).astype(BF)
    wrow = wids[...]
    eye = iota((128, 128), 0) == iota((128, 128), 1)
    wcol = jnp.sum(jnp.where(eye, wrow, 0).astype(F32), axis=1, keepdims=True)
    scores = nt(vq, vk) / math.sqrt(VHD)
    scores = jnp.where(wcol == wrow.astype(F32), scores, big_negative)
    powers = jnp.exp(scores - jnp.max(scores, axis=-1, keepdims=True))
    totals = jnp.sum(powers, axis=-1, keepdims=True)
    blended = (nn(powers.astype(BF), vv) / totals).astype(BF)
    perm1 = hot(iota((128, 128), 1) == 4 * lax.rem(iota((128, 128), 0), 32) + iota((128, 128), 0) // 32)
    blp[...] = nn(perm1, blended).astype(BF).reshape(8, 16, VHD)
    pp[...] = nn(perm1, patch[...]).astype(BF).reshape(8, 16, VD)
    mixb[t, x] = blp[x * 2 + t]
    res[x] = pp[x * 2 + t]

    pl.semaphore_wait(barrier, greetings)

    x1 = []
    for k in range(NX):
        for dt in range(NT):
            if k + dt:
                tt = t if dt == 0 else other
                xx = lax.rem(x + k, NX)
                n = k * 2 + dt
                x1.append(remote(blp.at[xx * 2 + tt], mixb.at[t, x], x1s.at[n], x1r.at[n], at_x(k, tt)))
    for cp in x1:
        cp.start()
    for load in loads[2:]:
        load.wait()
    vo_cp = remote(vo.at[t], vo.at[t], vos, vor, partner)
    vo_cp.start()
    res_cp = []
    for k in range(1, NX):
        res_cp.append(remote(pp.at[lax.rem(x + k, NX) * 2 + t], res.at[x], ress.at[k], resr.at[k], at_x(k, t)))
        res_cp[-1].start()
    w_cp = [remote(wbuf.at[y], wbuf.at[y], ws.at[k], wr.at[k], at_y(k)) for k in range(1, NY)]
    for cp in w_cp:
        cp.start()
    t_cp = [remote(tbuf.at[t, v], tbuf.at[t, v], ts.at[k], tr.at[k], at_v(k)) for k in range(1, NV)]
    for cp in t_cp:
        cp.start()

    for cp in x1:
        cp.wait_recv()
    vo_cp.wait_recv()
    r64, c64 = iota((64, 64), 0), iota((64, 64), 1)
    perm2 = hot(c64 == (lax.rem(r64, 8) // 2) * 16 + (r64 // 8) * 2 + lax.rem(r64, 2))
    m0 = nn(perm2, mixb[0].reshape(64, VHD)).astype(BF)
    m1 = nn(perm2, mixb[1].reshape(64, VHD)).astype(BF)
    part = nn(m0, vo[0]) + nn(m1, vo[1])
    for k in range(NV):
        rs_src[k] = fold(part[8 * k : 8 * k + 8]).astype(BF)
    rs_cp = []
    for k in range(1, NV):
        cp = remote(rs_src.at[lax.rem(v + k, NV)], rs_buf.at[v], rss.at[k], rsr.at[k], at_v(k))
        cp.start()
        rs_cp.append(cp)
    rs_buf[v] = rs_src[v]

    for load in loads[:2]:
        load.wait()
    r256, c256 = iota((256, 256), 0), iota((256, 256), 1)
    perm_w = hot(c256 == 2 * lax.rem(r256, 128) + r256 // 128)

    def split_w(i, z):
        both = nn(perm_w, wq_land[pl.ds(pl.multiple_of(i * 256, 256), 256), :]).astype(BF)
        at = pl.ds(pl.multiple_of(i * 128, 128), 128)
        wq[at, 0:128] = both[:128]
        wq[at, 128:256] = both[128:]
        return z

    lax.fori_loop(0, 32, split_w, 0)

    for cp in res_cp:
        cp.wait_recv()
    pick = hot(iota((8, 64), 1) == (iota((8, 64), 0) // 2) * 16 + 2 * v + lax.rem(iota((8, 64), 0), 2))
    residual = nn(pick, res[...].reshape(64, VD))
    for cp in rs_cp:
        cp.wait_recv()
    summed = rs_buf[0].astype(F32)
    for k in range(1, NV):
        summed = summed + rs_buf[k].astype(F32)
    hidden = residual + unfold(summed)
    merged8 = layer_norm(hidden, mgain[...], mbias[...])
    ag[t, v] = fold(merged8).astype(BF)
    ag_cp = [remote(ag.at[t, v], ag.at[t, v], ags.at[k], agr.at[k], at_v(k)) for k in range(1, NV)]
    for cp in ag_cp:
        cp.start()

    for cp in t_cp:
        cp.wait_recv()
    t_fwd = remote(tbuf.at[t], tbuf.at[t], fs.at[0], fr.at[0], partner)
    t_fwd.start()

    s_own = sorder[c]
    slices = (s_own, 2 * NC - 1 - s_own)
    ip = ipos[...]
    lane1024 = iota((1, 1024), 1)
    ishard = lane1024 // 32
    patches = jnp.sum(ipatch[...].astype(F32), axis=0, keepdims=True)
    eye32 = iota((32, 32), 0) == iota((32, 32), 1)
    pcol = jnp.sum(jnp.where(eye32, patches, 0.0), axis=1, keepdims=True)
    live_all = (ishard == iota((32, 1024), 0)) & ((4 * lax.rem(lane1024, 32)).astype(F32) < pcol)
    live = jnp.sum(jnp.where(live_all, 1.0, 0.0), axis=0, keepdims=True)
    ipf = ip.astype(F32)
    rows_col = iota((128, 1), 0)
    own_pos = jnp.where(rows_col < 64, slices[0] * 64, slices[1] * 64) + lax.rem(rows_col, 64)
    own_pos_f = own_pos.astype(F32)
    hit = jnp.where((own_pos == ip) & (live > 0.5), 1.0, 0.0)
    is_image = jnp.sum(hit, axis=1, keepdims=True) > 0.5
    gather32 = hot(iota((1024, 32), 0) // 32 == iota((1024, 32), 1))
    place = nn(hit.astype(BF), gather32).astype(BF)
    own_doc = jnp.zeros((128, 128), F32)
    for j in range(32):
        blk = docs[:, 128 * j : 128 * j + 128].astype(F32)
        own_doc = own_doc + jnp.where(own_pos == iota((1, 128), 1) + 128 * j, blk, 0.0)
    own_doc = jnp.sum(own_doc, axis=1, keepdims=True)
    below = jnp.zeros((128, 128), F32)
    for j in range(32):
        blk = docs[:, 128 * j : 128 * j + 128].astype(F32)
        below = below + jnp.where(blk < own_doc, 1.0, 0.0)
    low = jnp.sum(below, axis=1, keepdims=True)
    own_slot = lane1024 == c * 32 + iota((32, 1024), 0)
    own_ipos = jnp.sum(jnp.where(own_slot, ipf, 0.0), axis=1, keepdims=True)
    so_col = jnp.sum(jnp.where(eye32, sorder_v[...].astype(F32), 0.0), axis=1, keepdims=True)
    sl = ip // 64
    pair = jnp.minimum(sl, 2 * NC - 1 - sl).astype(F32)
    goes = hot((pair == so_col) & (ishard == c))
    in_off = hot(lax.rem(ip, 64) == iota((64, 1024), 0))
    low_half = nt(hot((sl.astype(F32) == so_col) & (live > 0.5)), in_off)
    high_half = nt(hot((sl.astype(F32) == 2 * NC - 1 - so_col) & (live > 0.5)), in_off)
    gone = jnp.concatenate([low_half, high_half], axis=1)
    offset = iota((1, 128), 1)
    shard_pos = jnp.where(offset < 64, so_col * 64, (2 * NC - 1 - so_col) * 64) + lax.rem(offset, 64).astype(F32)
    shard_pos = jnp.where(gone > 0.5, 1e9, shard_pos)
    for e in range(NC):
        kpos_s[:, 128 * e : 128 * e + 128] = shard_pos[e : e + 1]
    ipos_live = jnp.where(live > 0.5, ipf, 1e9)
    gather32_t = hot(iota((32, 1024), 1) // 32 == iota((32, 1024), 0))
    place_t = nt(gather32_t, hit.astype(BF)) > 0.5
    low_row = jnp.sum(jnp.where(eye, low, 0.0), axis=0, keepdims=True)
    pos_row = jnp.sum(jnp.where(eye, own_pos_f, 0.0), axis=0, keepdims=True)
    low_i = jnp.sum(jnp.where(place_t, low_row, 0.0), axis=1, keepdims=True)
    pos_i = jnp.sum(jnp.where(place_t, pos_row, 0.0), axis=1, keepdims=True)
    fold32 = hot(lax.rem(iota((1024, 32), 0), 32) == iota((1024, 32), 1))
    select = nn(goes, fold32).astype(BF)
    cos_t, sin_t = angles_of(own_pos_f, freq[...])
    cos_i, sin_i = angles_of(own_ipos, freq[...])

    for cp in ag_cp:
        cp.wait_recv()
    ag_fwd = remote(ag.at[t], ag.at[t], fs.at[1], fr.at[1], partner)
    ag_fwd.start()
    for cp in w_cp:
        cp.wait_recv()
    ag_fwd.wait_recv()
    half_of, rest = r256 // 128, lax.rem(r256, 128)
    xs, j = rest // 32, lax.rem(rest, 32)
    perm3 = hot(c256 == (j // 16) * 128 + (lax.rem(j, 16) // 2) * 16 + half_of * 8 + xs * 2 + lax.rem(j, 2))
    mp = nn(perm3, ag[...].reshape(256, 640)).astype(BF)
    wg = wbuf[...].reshape(VD, 256)
    yv = nn(mp[:128], wg[:640]) + nn(mp[128:], wg[640:])
    ysrc[...] = yv.reshape(NX, 32, 256)
    y_cp = []
    for k in range(1, NX):
        cp = remote(ysrc.at[lax.rem(x + k, NX)], ybuf.at[x], ys.at[k], yr.at[k], at_x(k, t))
        cp.start()
        y_cp.append(cp)
    ybuf[x] = ysrc[x]

    t_fwd.wait_recv()

    def normalise(buf, dst, rows):
        def squares(i, total):
            blk = buf[lax.rem(i, 2), i // 2].astype(F32)
            return total + jnp.sum(blk * blk, axis=1, keepdims=True)

        total = lax.fori_loop(0, 16, squares, jnp.zeros((rows, 1), F32))
        scale = lax.rsqrt(total * (1.0 / D) + norm_eps)
        for i in range(16):
            cols = slice(256 * i, 256 * i + 256)
            dst[:, cols] = (buf[i % 2, i // 2].astype(F32) * scale * ngain[:, cols]).astype(BF)

    normalise(tbuf, ntext, TOK)
    kv_t = nn(ntext[...], wkv[...])
    kvbuf[t, c] = jnp.where(t == 0, rotate(kv_t, cos_t, sin_t), kv_t).astype(BF)

    def kv_copy(k):
        return remote(kvbuf.at[t, c], kvbuf.at[t, c], kvs.at[k], kvr.at[k], at_c(k))

    lax.fori_loop(1, NC, lambda k, z: (kv_copy(k).start(), z)[1], 0)

    for cp in y_cp:
        cp.wait_recv()
    emb = ybuf[0]
    for k in range(1, NX):
        emb = emb + ybuf[k]
    p4[t, v] = emb.astype(BF)
    p4_cp = [remote(p4.at[t, v], p4.at[t, v], p4s.at[k], p4r.at[k], at_v(k)) for k in range(1, NV)]
    for cp in p4_cp:
        cp.start()
    q_t = nn(ntext[...], wq[...])
    q_t = [rotate(q_t[:, :128], cos_t, sin_t).astype(BF), rotate(q_t[:, 128:], cos_t, sin_t).astype(BF)]

    for cp in p4_cp:
        cp.wait_recv()
    p4_fwd = remote(p4.at[t], p4.at[t], fs.at[2], fr.at[2], partner)
    p4_fwd.start()
    p4_fwd.wait_recv()
    normalise(p4, nimg, 32)
    q_i = nn(nimg[...], wq[...])
    q_i = jnp.concatenate(
        [rotate(q_i[:, :128], cos_i, sin_i), rotate(q_i[:, 128:], cos_i, sin_i)], axis=1
    ).astype(BF)
    q_go = nn(select, q_i)
    for e in range(NC):
        qsrc[e] = q_go[e : e + 1]
    qbuf[c] = qsrc[c]

    def q_copy(k):
        return remote(qsrc.at[lax.rem(c + k, NC)], qbuf.at[c], qs.at[k], qr.at[k], at_c(k))

    kv_i = nn(nimg[...], wkv[...])
    kibuf[t, c] = jnp.where(t == 0, rotate(kv_i, cos_i, sin_i), kv_i).astype(BF)

    def ki_copy(k):
        return remote(kibuf.at[t, c], kibuf.at[t, c], kis.at[k], kir.at[k], at_c(k))

    lax.fori_loop(1, NC, lambda k, z: (ki_copy(k).start(), z)[1], 0)
    lax.fori_loop(1, NC, lambda k, z: (q_copy(k).start(), z)[1], 0)

    lax.fori_loop(1, NC, lambda k, z: (kv_copy(k).wait_recv(), z)[1], 0)
    kv_fwd = remote(kvbuf.at[t], kvbuf.at[t], fs.at[3], fr.at[3], partner)
    kv_fwd.start()
    lax.fori_loop(1, NC, lambda k, z: (ki_copy(k).wait_recv(), z)[1], 0)
    ki_fwd = remote(kibuf.at[t], kibuf.at[t], fs.at[4], fr.at[4], partner)
    ki_fwd.start()
    lax.fori_loop(1, NC, lambda k, z: (q_copy(k).wait_recv(), z)[1], 0)
    q_in = jnp.concatenate([qbuf[e] for e in range(NC)], axis=0).astype(BF)
    kv_fwd.wait_recv()
    pos2, low2 = jnp.concatenate([own_pos_f] * 2, axis=0), jnp.concatenate([low] * 2, axis=0)
    pos2_i, low2_i = jnp.concatenate([pos_i] * 2, axis=0), jnp.concatenate([low_i] * 2, axis=0)
    qq = jnp.concatenate([q_t[0], q_t[1], q_in[:, :128], q_in[:, 128:]], axis=0)
    qq_pos = jnp.concatenate([pos2, pos2_i], axis=0)
    qq_low = jnp.concatenate([low2, low2_i], axis=0)
    scale = 1.0 / math.sqrt(HD)

    def attend(state, keys, values, kpos):
        best, total, acc = state
        s = nt(qq, keys) * scale
        s = jnp.where((kpos >= qq_low) & (kpos <= qq_pos), s, big_negative)
        new = jnp.maximum(best, jnp.max(s, axis=1, keepdims=True))
        factor = jnp.exp(best - new)
        p = jnp.exp(s - new)
        total = total * factor + jnp.sum(p, axis=1, keepdims=True)
        return new, total, acc * factor + nn(p.astype(BF), values)

    rows = qq.shape[0]
    state = (jnp.full((rows, 1), big_negative, F32), jnp.zeros((rows, 1), F32), jnp.zeros((rows, HD), F32))
    for b in range(4):
        keys = kvbuf[0, 8 * b : 8 * b + 8].reshape(1024, HD)
        values = kvbuf[1, 8 * b : 8 * b + 8].reshape(1024, HD)
        state = attend(state, keys, values, kpos_s[:, 1024 * b : 1024 * b + 1024])
    ki_fwd.wait_recv()
    state = attend(state, kibuf[0].reshape(1024, HD), kibuf[1].reshape(1024, HD), ipos_live)
    result = (state[2] / state[1]).astype(BF)
    for g in range(2):
        placed = nn(place, result[256 + 32 * g : 288 + 32 * g])
        mixed = jnp.where(is_image, placed, result[128 * g : 128 * g + 128].astype(F32))
        out[:, 128 * g : 128 * g + 128] = mixed.astype(BF)

    for cp in x1 + [vo_cp] + res_cp + w_cp + t_cp + rs_cp + ag_cp + y_cp + p4_cp:
        cp.wait_send()
    for cp in (t_fwd, ag_fwd, p4_fwd, kv_fwd, ki_fwd):
        cp.wait_send()
    lax.fori_loop(1, NC, lambda k, z: (kv_copy(k).wait_send(), ki_copy(k).wait_send(), q_copy(k).wait_send(), z)[3], 0)


def local(
    patch_rows, vit_gain, vit_bias, vit_qkv, vit_out, merge_gain, merge_bias, merge_weight,
    image_patches, window_ids, image_pos, slice_order, doc_ids, text_rows, norm_gain, w_query, w_keyval,
):
    exponent = np.arange(64, dtype=np.float64) * (-2.0 / HD)
    freq = np.power(np.float64(rope_base), exponent).astype(np.float32)
    freq = jnp.asarray(np.concatenate([freq, freq])[None, :])
    vm = pl.BlockSpec(memory_space=pltpu.VMEM)
    hbm = pl.BlockSpec(memory_space=pl.ANY)
    sm = pl.BlockSpec(memory_space=pltpu.SMEM)
    dma = pltpu.SemaphoreType.DMA
    args = [
        (patch_rows, vm),
        (vit_gain.reshape(1, VD), vm),
        (vit_bias.reshape(1, VD), vm),
        (jnp.transpose(vit_qkv, (1, 2, 3, 0)).reshape(3 * VHD, VD), vm),
        (vit_out.reshape(VHD, VD), hbm),
        (merge_gain.reshape(1, VD), vm),
        (merge_bias.reshape(1, VD), vm),
        (merge_weight, hbm),
        (jnp.transpose(image_patches), vm),
        (window_ids.reshape(1, 128), vm),
        (image_pos.reshape(1, 1024), vm),
        (slice_order, sm),
        (slice_order.reshape(1, NC), vm),
        (doc_ids.reshape(1, 4096), vm),
        (text_rows, hbm),
        (norm_gain.reshape(1, D), vm),
        (w_query.reshape(2 * D, HD), hbm),
        (w_keyval.reshape(D, HD), hbm),
        (freq, vm),
    ]
    scratch = [
        pltpu.VMEM((2 * D, HD), BF),
        pltpu.VMEM((D, 2 * HD), BF),
        pltpu.VMEM((D, HD), BF),
        pltpu.VMEM((NY, 160, 256), BF),
        pltpu.VMEM((NT, NV, TOK, 256), BF),
        pltpu.VMEM((TOK, D), BF),
        pltpu.VMEM((NT, NC, TOK, HD), BF),
        pltpu.VMEM((NT, NC, 32, HD), BF),
        pltpu.VMEM((8, 16, VHD), BF),
        pltpu.VMEM((NT, NX, 16, VHD), BF),
        pltpu.VMEM((NT, VHD, VD), BF),
        pltpu.VMEM((8, 16, VD), BF),
        pltpu.VMEM((NX, 16, VD), BF),
        pltpu.VMEM((NV, 16, 640), BF),
        pltpu.VMEM((NV, 16, 640), BF),
        pltpu.VMEM((NT, NV, 16, 640), BF),
        pltpu.VMEM((NX, 32, 256), F32),
        pltpu.VMEM((NX, 32, 256), F32),
        pltpu.VMEM((NT, NV, 32, 256), BF),
        pltpu.VMEM((32, D), BF),
        pltpu.VMEM((NC, 1, 256), F32),
        pltpu.VMEM((NC, 1, 256), F32),
        pltpu.VMEM((1, 4096), F32),
        dma((5,)),
        dma((8,)), dma((8,)),
        dma, dma,
        dma((NX,)), dma((NX,)),
        dma((NY,)), dma((NY,)),
        dma((NV,)), dma((NV,)),
        dma((NV,)), dma((NV,)),
        dma((NV,)), dma((NV,)),
        dma((NX,)), dma((NX,)),
        dma((NV,)), dma((NV,)),
        dma((NC,)), dma((NC,)),
        dma((NC,)), dma((NC,)),
        dma((NC,)), dma((NC,)),
        dma((5,)), dma((5,)),
    ]
    result = pl.pallas_call(
        kernel,
        name="fused",
        out_shape=jax.ShapeDtypeStruct((TOK, 256), BF),
        in_specs=[spec for _, spec in args],
        out_specs=vm,
        scratch_shapes=scratch,
        compiler_params=pltpu.CompilerParams(
            collective_id=0, has_side_effects=True, vmem_limit_bytes=48 << 20
        ),
    )(*[value for value, _ in args])
    return result.reshape(TOK, 1, 256)


def solution(mesh):
    placed = (
        P("ctx", None),
        P(),
        P(),
        P(None, None, ("vis", "tp"), None),
        P(("vis", "tp"), None, None),
        P(),
        P(),
        P("ctx", ("vis", "tp")),
        P(),
        P("ctx"),
        P(),
        P(),
        P(),
        P("ctx", ("vis", "tp")),
        P(),
        P(None, "vis", "tp", None),
        P("tp", None, "vis", None),
    )
    return jax.shard_map(
        local, mesh=mesh, in_specs=placed, out_specs=P("ctx", "vis", "tp"), check_vma=False
    )
```

```python
import functools
import math

import jax
import jax.numpy as jnp
import numpy as np
from jax import lax
from jax.experimental import pallas as pl
from jax.experimental.pallas import tpu as pltpu
from jax.sharding import PartitionSpec as P

D = 4096
HD = 128
VD = 1280
VHD = 80
TOK = 128
NV, NX, NY, NT = 8, 4, 8, 2
NC = NX * NY

norm_eps = 1e-06
rope_base = 1000000.0
big_negative = -1e30
MESH = pl.DeviceIdType.MESH
F32 = jnp.float32
BF = jnp.bfloat16


def nn(a, b):
    return lax.dot_general(a, b, (((1,), (0,)), ((), ())), preferred_element_type=F32)


def nt(a, b):
    return lax.dot_general(a, b, (((1,), (1,)), ((), ())), preferred_element_type=F32)


def iota(shape, dim):
    return lax.broadcasted_iota(jnp.int32, shape, dim)


def hot(mask):
    return jnp.where(mask, 1.0, 0.0).astype(BF)


def layer_norm(values, scale_vec, shift_vec):
    centre = jnp.mean(values, axis=-1, keepdims=True)
    offset = values - centre
    spread = jnp.mean(offset * offset, axis=-1, keepdims=True)
    return offset * lax.rsqrt(spread + norm_eps) * scale_vec + shift_vec


def rotate(values, cosine, sine):
    return values * cosine + pltpu.roll(values, 64, 1) * sine


def angles_of(pos_column, freq_row):
    ang = pos_column * freq_row
    sign = jnp.where(iota(ang.shape, 1) < 64, -1.0, 1.0)
    return jnp.cos(ang), jnp.sin(ang) * sign


def fold(rows8):
    return jnp.concatenate([rows8[:, :640], rows8[:, 640:]], axis=0)


def unfold(rows16):
    return jnp.concatenate([rows16[:8], rows16[8:]], axis=1)


def kernel(
    patch_h, vgain_h, vbias_h, wqkv_h, vout, mgain_h, mbias_h, wblk, ipatch_h, wids_h, ipos_h, sorder_h, docs_h,
    text, ngain_h, wq_raw, wkv_in, freq_h, out,
    patch, vgain, vbias, wqkv, mgain, mbias, ipatch, wids, ipos, sorder, sorder_v, docs, ngain, freq,
    wq_land, wq, wkv, wbuf, tbuf, ntext, kvbuf, kibuf, blp, mixb, vo, pp, res,
    rs_src, rs_buf, ag, ysrc, ybuf, p4, nimg, qsrc, qbuf, kpos_s,
    lsem, x1s, x1r, vos, vor, ress, resr, ws, wr, ts, tr, rss, rsr, ags, agr, ys, yr,
    p4s, p4r, kvs, kvr, kis, kir, qs, qr, fs, fr,
):
    v, c, t = lax.axis_index("vis"), lax.axis_index("ctx"), lax.axis_index("tp")
    x, y = c // NY, lax.rem(c, NY)
    other = 1 - t

    def at_v(k):
        return (lax.rem(v + k, NV), c, t)

    def at_c(k):
        return (v, lax.rem(c + k, NC), t)

    def at_y(k):
        return (v, x * NY + lax.rem(y + k, NY), t)

    def at_x(k, tt):
        return (v, lax.rem(x + k, NX) * NY + y, tt)

    partner = (v, c, other)

    pairs = [
        (patch_h, patch), (vgain_h, vgain), (vbias_h, vbias), (wqkv_h, wqkv), (wids_h, wids),
        (vout, vo.at[t]), (text, tbuf.at[t, v]), (wblk, wbuf.at[y]),
        (wq_raw, wq_land), (mgain_h, mgain), (mbias_h, mbias), (ipatch_h, ipatch), (ipos_h, ipos),
        (sorder_h, sorder_v), (sorder_h, sorder), (docs_h, docs), (ngain_h, ngain), (freq_h, freq), (wkv_in, wkv),
    ]
    loads = [pltpu.make_async_copy(a, b, lsem.at[n]) for n, (a, b) in enumerate(pairs)]
    for load in loads:
        load.start()

    barrier = pltpu.get_barrier_semaphore()

    def greet(d):
        pl.semaphore_signal(barrier, inc=1, device_id=d, device_id_type=MESH)

    lax.fori_loop(1, NV, lambda k, z: (greet(at_v(k)), z)[1], 0)
    lax.fori_loop(1, NC, lambda k, z: (greet(at_c(k)), z)[1], 0)
    for k in range(1, NX):
        greet(at_x(k, other))
    greet(partner)
    greetings = (NV - 1) + (NC - 1) + (NX - 1) + 1


    def remote(src, dst, ssem, rsem, d):
        return pltpu.make_async_remote_copy(
            src_ref=src, dst_ref=dst, send_sem=ssem, recv_sem=rsem, device_id=d, device_id_type=MESH
        )

    for load in loads[:5]:
        load.wait()
    normed = layer_norm(patch[...].astype(F32), vgain[...].reshape(1, VD), vbias[...].reshape(1, VD)).astype(BF)
    vq = nt(normed, wqkv[0:80, :]).astype(BF)
    vk = nt(normed, wqkv[80:160, :]).astype(BF)
    vv = nt(normed, wqkv[160:240, :]).astype(BF)
    wrow = wids[...]
    eye = iota((128, 128), 0) == iota((128, 128), 1)
    wcol = jnp.sum(jnp.where(eye, wrow, 0).astype(F32), axis=1, keepdims=True)
    scores = nt(vq, vk) / math.sqrt(VHD)
    scores = jnp.where(wcol == wrow.astype(F32), scores, big_negative)
    powers = jnp.exp(scores - jnp.max(scores, axis=-1, keepdims=True))
    totals = jnp.sum(powers, axis=-1, keepdims=True)
    blended = (nn(powers.astype(BF), vv) / totals).astype(BF)
    perm1 = hot(iota((128, 128), 1) == 4 * lax.rem(iota((128, 128), 0), 32) + iota((128, 128), 0) // 32)
    blp[...] = nn(perm1, blended).astype(BF).reshape(8, 16, VHD)
    pp[...] = nn(perm1, patch[...]).astype(BF).reshape(8, 16, VD)
    mixb[t, x] = blp[x * 2 + t]
    res[x] = pp[x * 2 + t]

    pl.semaphore_wait(barrier, greetings)

    x1 = []
    for k in range(NX):
        for dt in range(NT):
            if k + dt:
                tt = t if dt == 0 else other
                xx = lax.rem(x + k, NX)
                n = k * 2 + dt
                x1.append(remote(blp.at[xx * 2 + tt], mixb.at[t, x], x1s.at[n], x1r.at[n], at_x(k, tt)))
    for cp in x1:
        cp.start()
    for load in loads[5:8]:
        load.wait()
    vo_cp = remote(vo.at[t], vo.at[t], vos, vor, partner)
    vo_cp.start()
    res_cp = []
    for k in range(1, NX):
        res_cp.append(remote(pp.at[lax.rem(x + k, NX) * 2 + t], res.at[x], ress.at[k], resr.at[k], at_x(k, t)))
        res_cp[-1].start()
    t_cp = {
        k: remote(tbuf.at[t, v], tbuf.at[t, v], ts.at[k], tr.at[k], at_v(k)) for k in range(1, NV)
    }
    for k in (1, 7, 2, 6):
        t_cp[k].start()
    w_cp = [remote(wbuf.at[y], wbuf.at[y], ws.at[k], wr.at[k], at_y(k)) for k in range(1, NY)]
    for cp in w_cp:
        cp.start()
    for cp in x1:
        cp.wait_recv()
    vo_cp.wait_recv()
    r64, c64 = iota((64, 64), 0), iota((64, 64), 1)
    perm2 = hot(c64 == (lax.rem(r64, 8) // 2) * 16 + (r64 // 8) * 2 + lax.rem(r64, 2))
    m0 = nn(perm2, mixb[0].reshape(64, VHD)).astype(BF)
    m1 = nn(perm2, mixb[1].reshape(64, VHD)).astype(BF)
    part = nn(m0, vo[0]) + nn(m1, vo[1])
    for k in range(NV):
        rs_src[k] = fold(part[8 * k : 8 * k + 8]).astype(BF)
    rs_cp = []
    for k in range(1, NV):
        cp = remote(rs_src.at[lax.rem(v + k, NV)], rs_buf.at[v], rss.at[k], rsr.at[k], at_v(k))
        cp.start()
        rs_cp.append(cp)
    rs_buf[v] = rs_src[v]
    for k in (3, 5, 4):
        t_cp[k].start()

    for load in loads[8:]:
        load.wait()
    r256, c256 = iota((256, 256), 0), iota((256, 256), 1)
    perm_w = hot(c256 == 2 * lax.rem(r256, 128) + r256 // 128)

    def split_w(i, z):
        both = nn(perm_w, wq_land[pl.ds(pl.multiple_of(i * 256, 256), 256), :]).astype(BF)
        at = pl.ds(pl.multiple_of(i * 128, 128), 128)
        wq[at, 0:128] = both[:128]
        wq[at, 128:256] = both[128:]
        return z

    lax.fori_loop(0, 32, split_w, 0)

    s_own = sorder[0, c]
    slices = (s_own, 2 * NC - 1 - s_own)
    ip = ipos[...]
    lane1024 = iota((1, 1024), 1)
    ishard = lane1024 // 32
    patches = jnp.sum(ipatch[...].astype(F32), axis=0, keepdims=True)
    eye32 = iota((32, 32), 0) == iota((32, 32), 1)
    pcol = jnp.sum(jnp.where(eye32, patches, 0.0), axis=1, keepdims=True)
    live_all = (ishard == iota((32, 1024), 0)) & ((4 * lax.rem(lane1024, 32)).astype(F32) < pcol)
    live = jnp.sum(jnp.where(live_all, 1.0, 0.0), axis=0, keepdims=True)
    ipf = ip.astype(F32)
    rows_col = iota((128, 1), 0)
    own_pos = jnp.where(rows_col < 64, slices[0] * 64, slices[1] * 64) + lax.rem(rows_col, 64)
    own_pos_f = own_pos.astype(F32)
    hit = jnp.where((own_pos == ip) & (live > 0.5), 1.0, 0.0)
    is_image = jnp.sum(hit, axis=1, keepdims=True) > 0.5
    gather32 = hot(iota((1024, 32), 0) // 32 == iota((1024, 32), 1))
    place = nn(hit.astype(BF), gather32).astype(BF)
    own_doc = jnp.zeros((128, 128), F32)
    for j in range(32):
        blk = docs[:, 128 * j : 128 * j + 128].astype(F32)
        own_doc = own_doc + jnp.where(own_pos == iota((1, 128), 1) + 128 * j, blk, 0.0)
    own_doc = jnp.sum(own_doc, axis=1, keepdims=True)
    below = jnp.zeros((128, 128), F32)
    for j in range(32):
        blk = docs[:, 128 * j : 128 * j + 128].astype(F32)
        below = below + jnp.where(blk < own_doc, 1.0, 0.0)
    low = jnp.sum(below, axis=1, keepdims=True)
    own_slot = lane1024 == c * 32 + iota((32, 1024), 0)
    own_ipos = jnp.sum(jnp.where(own_slot, ipf, 0.0), axis=1, keepdims=True)
    so_col = jnp.sum(jnp.where(eye32, sorder_v[...].astype(F32), 0.0), axis=1, keepdims=True)
    sl = ip // 64
    pair = jnp.minimum(sl, 2 * NC - 1 - sl).astype(F32)
    goes = hot((pair == so_col) & (ishard == c))
    in_off = hot(lax.rem(ip, 64) == iota((64, 1024), 0))
    low_half = nt(hot((sl.astype(F32) == so_col) & (live > 0.5)), in_off)
    high_half = nt(hot((sl.astype(F32) == 2 * NC - 1 - so_col) & (live > 0.5)), in_off)
    gone = jnp.concatenate([low_half, high_half], axis=1)
    offset = iota((1, 128), 1)
    shard_pos = jnp.where(offset < 64, so_col * 64, (2 * NC - 1 - so_col) * 64) + lax.rem(offset, 64).astype(F32)
    shard_pos = jnp.where(gone > 0.5, 1e9, shard_pos)
    for e in range(NC):
        kpos_s[e // 8, :, 128 * (e % 8) : 128 * (e % 8) + 128] = shard_pos[e : e + 1]
    ipos_live = jnp.where(live > 0.5, ipf, 1e9)
    gather32_t = hot(iota((32, 1024), 1) // 32 == iota((32, 1024), 0))
    place_t = nt(gather32_t, hit.astype(BF)) > 0.5
    low_row = jnp.sum(jnp.where(eye, low, 0.0), axis=0, keepdims=True)
    pos_row = jnp.sum(jnp.where(eye, own_pos_f, 0.0), axis=0, keepdims=True)
    low_i = jnp.sum(jnp.where(place_t, low_row, 0.0), axis=1, keepdims=True)
    pos_i = jnp.sum(jnp.where(place_t, pos_row, 0.0), axis=1, keepdims=True)
    fold32 = hot(lax.rem(iota((1024, 32), 0), 32) == iota((1024, 32), 1))
    select = nn(goes, fold32).astype(BF)
    cos_t, sin_t = angles_of(own_pos_f, freq[...])
    cos_i, sin_i = angles_of(own_ipos, freq[...])

    for cp in res_cp:
        cp.wait_recv()
    pick = hot(iota((8, 64), 1) == (iota((8, 64), 0) // 2) * 16 + 2 * v + lax.rem(iota((8, 64), 0), 2))
    residual = nn(pick, res[...].reshape(64, VD))
    for cp in rs_cp:
        cp.wait_recv()
    summed = rs_buf[0].astype(F32)
    for k in range(1, NV):
        summed = summed + rs_buf[k].astype(F32)
    hidden = residual + unfold(summed)
    merged8 = layer_norm(hidden, mgain[...].reshape(1, VD), mbias[...].reshape(1, VD))
    ag[t, v] = fold(merged8).astype(BF)
    ag_cp = [remote(ag.at[t, v], ag.at[t, v], ags.at[k], agr.at[k], at_v(k)) for k in range(1, NV)]
    for cp in ag_cp:
        cp.start()

    for k in range(1, NV):
        t_cp[k].wait_recv()
    t_fwd = remote(tbuf.at[t], tbuf.at[t], fs.at[0], fr.at[0], partner)
    t_fwd.start()
    t_fwd.wait_recv()

    def normalise(buf, dst, rows):
        def squares(i, total):
            blk = buf[lax.rem(i, 2), i // 2].astype(F32)
            return total + jnp.sum(blk * blk, axis=1, keepdims=True)

        total = lax.fori_loop(0, 16, squares, jnp.zeros((rows, 1), F32))
        scale = lax.rsqrt(total * (1.0 / D) + norm_eps)
        for i in range(16):
            cols = slice(256 * i, 256 * i + 256)
            dst[:, cols] = (buf[i % 2, i // 2].astype(F32) * scale * ngain[:, cols]).astype(BF)

    normalise(tbuf, ntext, TOK)
    kv_t = nn(ntext[...], wkv[...])
    kvbuf[t, c] = jnp.where(t == 0, rotate(kv_t, cos_t, sin_t), kv_t).astype(BF)

    def kv_copy(k):
        return remote(kvbuf.at[t, c], kvbuf.at[t, c], kvs.at[k], kvr.at[k], at_c(k))

    lax.fori_loop(1, NC, lambda k, z: (kv_copy(k).start(), z)[1], 0)

    for cp in ag_cp:
        cp.wait_recv()
    ag_fwd = remote(ag.at[t], ag.at[t], fs.at[1], fr.at[1], partner)
    ag_fwd.start()
    for cp in w_cp:
        cp.wait_recv()
    ag_fwd.wait_recv()
    half_of, rest = r256 // 128, lax.rem(r256, 128)
    xs, j = rest // 32, lax.rem(rest, 32)
    perm3 = hot(c256 == (j // 16) * 128 + (lax.rem(j, 16) // 2) * 16 + half_of * 8 + xs * 2 + lax.rem(j, 2))
    mp = nn(perm3, ag[...].reshape(256, 640)).astype(BF)
    wg = wbuf[...].reshape(VD, 256)
    yv = nn(mp[:128], wg[:640]) + nn(mp[128:], wg[640:])
    ysrc[...] = yv.reshape(NX, 32, 256)
    y_cp = []
    for k in range(1, NX):
        cp = remote(ysrc.at[lax.rem(x + k, NX)], ybuf.at[x], ys.at[k], yr.at[k], at_x(k, t))
        cp.start()
        y_cp.append(cp)
    ybuf[x] = ysrc[x]

    for cp in y_cp:
        cp.wait_recv()
    emb = ybuf[0]
    for k in range(1, NX):
        emb = emb + ybuf[k]
    p4[t, v] = emb.astype(BF)
    p4_cp = [remote(p4.at[t, v], p4.at[t, v], p4s.at[k], p4r.at[k], at_v(k)) for k in range(1, NV)]
    for cp in p4_cp:
        cp.start()
    q_t = nn(ntext[...], wq[...])
    q_t = [rotate(q_t[:, :128], cos_t, sin_t).astype(BF), rotate(q_t[:, 128:], cos_t, sin_t).astype(BF)]

    for cp in p4_cp:
        cp.wait_recv()
    p4_fwd = remote(p4.at[t], p4.at[t], fs.at[2], fr.at[2], partner)
    p4_fwd.start()
    p4_fwd.wait_recv()
    normalise(p4, nimg, 32)
    q_i = nn(nimg[...], wq[...])
    q_i = jnp.concatenate(
        [rotate(q_i[:, :128], cos_i, sin_i), rotate(q_i[:, 128:], cos_i, sin_i)], axis=1
    ).astype(BF)
    q_go = nn(select, q_i)
    for e in range(NC):
        qsrc[e] = q_go[e : e + 1]
    qbuf[c] = qsrc[c]

    def q_copy(k):
        return remote(qsrc.at[lax.rem(c + k, NC)], qbuf.at[c], qs.at[k], qr.at[k], at_c(k))

    kv_i = nn(nimg[...], wkv[...])
    kibuf[t, c] = jnp.where(t == 0, rotate(kv_i, cos_i, sin_i), kv_i).astype(BF)

    def ki_copy(k):
        return remote(kibuf.at[t, c], kibuf.at[t, c], kis.at[k], kir.at[k], at_c(k))

    lax.fori_loop(1, NC, lambda k, z: (ki_copy(k).start(), z)[1], 0)
    lax.fori_loop(1, NC, lambda k, z: (q_copy(k).start(), z)[1], 0)

    lax.fori_loop(1, NC, lambda k, z: (kv_copy(k).wait_recv(), z)[1], 0)
    kv_fwd = remote(kvbuf.at[t], kvbuf.at[t], fs.at[3], fr.at[3], partner)
    kv_fwd.start()
    kv_fwd.wait_recv()
    scale = 1.0 / math.sqrt(HD)

    def attend(state, queries, qpos, qlow, keys, values, kpos):
        best, total, acc = state
        sc = nt(queries, keys) * scale
        sc = jnp.where((kpos >= qlow) & (kpos <= qpos), sc, big_negative)
        new = jnp.maximum(best, jnp.max(sc, axis=1, keepdims=True))
        factor = jnp.exp(best - new)
        p = jnp.exp(sc - new)
        total = total * factor + jnp.sum(p, axis=1, keepdims=True)
        return new, total, acc * factor + nn(p.astype(BF), values)

    def over_text(queries, qpos, qlow):
        rows = queries.shape[0]
        state = (jnp.full((rows, 1), big_negative, F32), jnp.zeros((rows, 1), F32), jnp.zeros((rows, HD), F32))

        def block(b, state):
            at = pl.ds(b * 8, 8)
            keys = kvbuf[0, at].reshape(1024, HD)
            values = kvbuf[1, at].reshape(1024, HD)
            return attend(state, queries, qpos, qlow, keys, values, kpos_s[b])

        return lax.fori_loop(0, 4, block, state)

    queries_t = jnp.concatenate(q_t, axis=0)
    pos2, low2 = jnp.concatenate([own_pos_f] * 2, axis=0), jnp.concatenate([low] * 2, axis=0)
    state_t = over_text(queries_t, pos2, low2)

    lax.fori_loop(1, NC, lambda k, z: (ki_copy(k).wait_recv(), z)[1], 0)
    ki_fwd = remote(kibuf.at[t], kibuf.at[t], fs.at[4], fr.at[4], partner)
    ki_fwd.start()
    lax.fori_loop(1, NC, lambda k, z: (q_copy(k).wait_recv(), z)[1], 0)
    q_in = jnp.concatenate([qbuf[e] for e in range(NC)], axis=0).astype(BF)
    queries_i = jnp.concatenate([q_in[:, :128], q_in[:, 128:]], axis=0)
    pos2_i, low2_i = jnp.concatenate([pos_i] * 2, axis=0), jnp.concatenate([low_i] * 2, axis=0)
    state_i = over_text(queries_i, pos2_i, low2_i)
    ki_fwd.wait_recv()
    state = attend(
        [jnp.concatenate(parts, axis=0) for parts in zip(state_t, state_i, strict=True)],
        jnp.concatenate([queries_t, queries_i], axis=0),
        jnp.concatenate([pos2, pos2_i], axis=0),
        jnp.concatenate([low2, low2_i], axis=0),
        kibuf[0].reshape(1024, HD),
        kibuf[1].reshape(1024, HD),
        ipos_live,
    )
    result = (state[2] / state[1]).astype(BF)
    for g in range(2):
        placed = nn(place, result[256 + 32 * g : 288 + 32 * g])
        mixed = jnp.where(is_image, placed, result[128 * g : 128 * g + 128].astype(F32))
        out[:, 128 * g : 128 * g + 128] = mixed.astype(BF)

    for cp in x1 + [vo_cp] + res_cp + w_cp + list(t_cp.values()) + rs_cp + ag_cp + y_cp + p4_cp:
        cp.wait_send()
    for cp in (t_fwd, ag_fwd, p4_fwd, kv_fwd, ki_fwd):
        cp.wait_send()
    lax.fori_loop(1, NC, lambda k, z: (kv_copy(k).wait_send(), ki_copy(k).wait_send(), q_copy(k).wait_send(), z)[3], 0)


def local(
    patch_rows, vit_gain, vit_bias, vit_qkv, vit_out, merge_gain, merge_bias, merge_weight,
    image_patches, window_ids, image_pos, slice_order, doc_ids, text_rows, norm_gain, w_query, w_keyval,
):
    exponent = np.arange(64, dtype=np.float64) * (-2.0 / HD)
    freq = np.power(np.float64(rope_base), exponent).astype(np.float32)
    freq = jnp.asarray(np.concatenate([freq, freq])[None, :])
    vm = pl.BlockSpec(memory_space=pltpu.VMEM)
    dma = pltpu.SemaphoreType.DMA
    args = [
        patch_rows,
        vit_gain,
        vit_bias,
        jnp.transpose(vit_qkv, (1, 2, 3, 0)).reshape(3 * VHD, VD),
        vit_out.reshape(VHD, VD),
        merge_gain,
        merge_bias,
        merge_weight,
        jnp.transpose(image_patches),
        window_ids.reshape(1, 128),
        image_pos.reshape(1, 1024),
        slice_order.reshape(1, NC),
        doc_ids.reshape(1, 4096),
        text_rows,
        norm_gain.reshape(1, D),
        w_query.reshape(2 * D, HD),
        w_keyval.reshape(D, HD),
        freq,
    ]
    scratch = [
        pltpu.VMEM((128, VD), BF),
        pltpu.VMEM((VD,), F32),
        pltpu.VMEM((VD,), F32),
        pltpu.VMEM((3 * VHD, VD), BF),
        pltpu.VMEM((VD,), F32),
        pltpu.VMEM((VD,), F32),
        pltpu.VMEM((2, NC), jnp.int32),
        pltpu.VMEM((1, 128), jnp.int32),
        pltpu.VMEM((1, 1024), jnp.int32),
        pltpu.SMEM((1, NC), jnp.int32),
        pltpu.VMEM((1, NC), jnp.int32),
        pltpu.VMEM((1, 4096), jnp.int32),
        pltpu.VMEM((1, D), F32),
        pltpu.VMEM((1, HD), F32),
        pltpu.VMEM((2 * D, HD), BF),
        pltpu.VMEM((D, 2 * HD), BF),
        pltpu.VMEM((D, HD), BF),
        pltpu.VMEM((NY, 160, 256), BF),
        pltpu.VMEM((NT, NV, TOK, 256), BF),
        pltpu.VMEM((TOK, D), BF),
        pltpu.VMEM((NT, NC, TOK, HD), BF),
        pltpu.VMEM((NT, NC, 32, HD), BF),
        pltpu.VMEM((8, 16, VHD), BF),
        pltpu.VMEM((NT, NX, 16, VHD), BF),
        pltpu.VMEM((NT, VHD, VD), BF),
        pltpu.VMEM((8, 16, VD), BF),
        pltpu.VMEM((NX, 16, VD), BF),
        pltpu.VMEM((NV, 16, 640), BF),
        pltpu.VMEM((NV, 16, 640), BF),
        pltpu.VMEM((NT, NV, 16, 640), BF),
        pltpu.VMEM((NX, 32, 256), F32),
        pltpu.VMEM((NX, 32, 256), F32),
        pltpu.VMEM((NT, NV, 32, 256), BF),
        pltpu.VMEM((32, D), BF),
        pltpu.VMEM((NC, 1, 256), F32),
        pltpu.VMEM((NC, 1, 256), F32),
        pltpu.VMEM((4, 1, 1024), F32),
        dma((19,)),
        dma((8,)), dma((8,)),
        dma, dma,
        dma((NX,)), dma((NX,)),
        dma((NY,)), dma((NY,)),
        dma((NV,)), dma((NV,)),
        dma((NV,)), dma((NV,)),
        dma((NV,)), dma((NV,)),
        dma((NX,)), dma((NX,)),
        dma((NV,)), dma((NV,)),
        dma((NC,)), dma((NC,)),
        dma((NC,)), dma((NC,)),
        dma((NC,)), dma((NC,)),
        dma((5,)), dma((5,)),
    ]
    result = pl.pallas_call(
        kernel,
        name="fused",
        out_shape=jax.ShapeDtypeStruct((TOK, 256), BF),
        in_specs=[pl.BlockSpec(memory_space=pl.ANY)] * len(args),
        out_specs=vm,
        scratch_shapes=scratch,
        compiler_params=pltpu.CompilerParams(
            collective_id=0, has_side_effects=True, vmem_limit_bytes=63 << 20
        ),
    )(*args)
    return result.reshape(TOK, 1, 256)


def solution(mesh):
    placed = (
        P("ctx", None),
        P(),
        P(),
        P(None, None, ("vis", "tp"), None),
        P(("vis", "tp"), None, None),
        P(),
        P(),
        P("ctx", ("vis", "tp")),
        P(),
        P("ctx"),
        P(),
        P(),
        P(),
        P("ctx", ("vis", "tp")),
        P(),
        P(None, "vis", "tp", None),
        P("tp", None, "vis", None),
    )
    return jax.shard_map(
        local, mesh=mesh, in_specs=placed, out_specs=P("ctx", "vis", "tp"), check_vma=False
    )
```

```python
import functools
import math

import jax
import jax.numpy as jnp
import numpy as np
from jax import lax
from jax.experimental import pallas as pl
from jax.experimental.pallas import tpu as pltpu
from jax.sharding import PartitionSpec as P

D = 4096
HD = 128
VD = 1280
VHD = 80
TOK = 128
NV, NX, NY, NT = 8, 4, 8, 2
NC = NX * NY

norm_eps = 1e-06
rope_base = 1000000.0
big_negative = -1e30
MESH = pl.DeviceIdType.MESH
F32 = jnp.float32
BF = jnp.bfloat16


def nn(a, b):
    return lax.dot_general(a, b, (((1,), (0,)), ((), ())), preferred_element_type=F32)


def nt(a, b):
    return lax.dot_general(a, b, (((1,), (1,)), ((), ())), preferred_element_type=F32)


def iota(shape, dim):
    return lax.broadcasted_iota(jnp.int32, shape, dim)


def hot(mask):
    return jnp.where(mask, 1.0, 0.0).astype(BF)


def layer_norm(values, scale_vec, shift_vec):
    centre = jnp.mean(values, axis=-1, keepdims=True)
    offset = values - centre
    spread = jnp.mean(offset * offset, axis=-1, keepdims=True)
    return offset * lax.rsqrt(spread + norm_eps) * scale_vec + shift_vec


def rotate(values, cosine, sine):
    return values * cosine + pltpu.roll(values, 64, 1) * sine


def angles_of(pos_column, freq_row):
    ang = pos_column * freq_row
    sign = jnp.where(iota(ang.shape, 1) < 64, -1.0, 1.0)
    return jnp.cos(ang), jnp.sin(ang) * sign


def fold(rows8):
    return jnp.concatenate([rows8[:, :640], rows8[:, 640:]], axis=0)


def unfold(rows16):
    return jnp.concatenate([rows16[:8], rows16[8:]], axis=1)


def kernel(
    patch_h, vgain_h, vbias_h, wqkv_h, vout, mgain_h, mbias_h, wblk, ipatch_h, wids_h, ipos_h, sorder_h, docs_h,
    text, ngain_h, wq_raw, wkv_in, freq_h, out,
    patch, vgain, vbias, wqkv, mgain, mbias, ipatch, wids, ipos, sorder, sorder_v, docs, ngain, freq,
    wq_land, wq, wkv, wbuf, tbuf, ntext, kvbuf, kibuf, blp, mixb, vo, pp, res,
    rs_src, rs_buf, ag, ysrc, ybuf, p4, nimg, qsrc, qbuf, kpos_s,
    lsem, x1s, x1r, vos, vor, ress, resr, ws, wr, ts, tr, rss, rsr, ags, agr, ys, yr,
    p4s, p4r, kvs, kvr, kis, kir, qs, qr, fs, fr,
):
    v, c, t = lax.axis_index("vis"), lax.axis_index("ctx"), lax.axis_index("tp")
    x, y = c // NY, lax.rem(c, NY)
    other = 1 - t

    def at_v(k):
        return (lax.rem(v + k, NV), c, t)

    def at_c(k):
        return (v, lax.rem(c + k, NC), t)

    def at_y(k):
        return (v, x * NY + lax.rem(y + k, NY), t)

    def at_x(k, tt):
        return (v, lax.rem(x + k, NX) * NY + y, tt)

    partner = (v, c, other)

    pairs = [
        (patch_h, patch), (vgain_h, vgain), (vbias_h, vbias), (wqkv_h, wqkv), (wids_h, wids),
        (vout, vo.at[t]), (text, tbuf.at[t, v]), (wblk, wbuf.at[y]),
        (wq_raw, wq_land), (mgain_h, mgain), (mbias_h, mbias), (ipatch_h, ipatch), (ipos_h, ipos),
        (sorder_h, sorder_v), (sorder_h, sorder), (docs_h, docs), (ngain_h, ngain), (freq_h, freq), (wkv_in, wkv),
    ]
    loads = [pltpu.make_async_copy(a, b, lsem.at[n]) for n, (a, b) in enumerate(pairs)]
    for load in loads:
        load.start()

    barrier = pltpu.get_barrier_semaphore()

    def greet(d):
        pl.semaphore_signal(barrier, inc=1, device_id=d, device_id_type=MESH)

    lax.fori_loop(1, NV, lambda k, z: (greet(at_v(k)), z)[1], 0)
    lax.fori_loop(1, NC, lambda k, z: (greet(at_c(k)), z)[1], 0)
    for k in range(1, NX):
        greet(at_x(k, other))
    greet(partner)
    greetings = (NV - 1) + (NC - 1) + (NX - 1) + 1


    def remote(src, dst, ssem, rsem, d):
        return pltpu.make_async_remote_copy(
            src_ref=src, dst_ref=dst, send_sem=ssem, recv_sem=rsem, device_id=d, device_id_type=MESH
        )

    for load in loads[:5]:
        load.wait()
    normed = layer_norm(patch[...].astype(F32), vgain[...].reshape(1, VD), vbias[...].reshape(1, VD)).astype(BF)
    vq = nt(normed, wqkv[0:80, :]).astype(BF)
    vk = nt(normed, wqkv[80:160, :]).astype(BF)
    vv = nt(normed, wqkv[160:240, :]).astype(BF)
    wrow = wids[...]
    eye = iota((128, 128), 0) == iota((128, 128), 1)
    wcol = jnp.sum(jnp.where(eye, wrow, 0).astype(F32), axis=1, keepdims=True)
    scores = nt(vq, vk) / math.sqrt(VHD)
    scores = jnp.where(wcol == wrow.astype(F32), scores, big_negative)
    powers = jnp.exp(scores - jnp.max(scores, axis=-1, keepdims=True))
    totals = jnp.sum(powers, axis=-1, keepdims=True)
    blended = (nn(powers.astype(BF), vv) / totals).astype(BF)
    perm1 = hot(iota((128, 128), 1) == 4 * lax.rem(iota((128, 128), 0), 32) + iota((128, 128), 0) // 32)
    blp[...] = nn(perm1, blended).astype(BF).reshape(8, 16, VHD)
    pp[...] = nn(perm1, patch[...]).astype(BF).reshape(8, 16, VD)
    mixb[t, x] = blp[x * 2 + t]
    res[x] = pp[x * 2 + t]

    pl.semaphore_wait(barrier, greetings)

    x1 = []
    for k in range(NX):
        for dt in range(NT):
            if k + dt:
                tt = t if dt == 0 else other
                xx = lax.rem(x + k, NX)
                n = k * 2 + dt
                x1.append(remote(blp.at[xx * 2 + tt], mixb.at[t, x], x1s.at[n], x1r.at[n], at_x(k, tt)))
    for cp in x1:
        cp.start()
    for load in loads[5:8]:
        load.wait()
    vo_cp = remote(vo.at[t], vo.at[t], vos, vor, partner)
    vo_cp.start()
    res_cp = []
    for k in range(1, NX):
        res_cp.append(remote(pp.at[lax.rem(x + k, NX) * 2 + t], res.at[x], ress.at[k], resr.at[k], at_x(k, t)))
        res_cp[-1].start()
    def t_copy(block, k, sem):
        blk = tbuf.at[t, lax.rem(v + block, NV)]
        return remote(blk, blk, ts.at[sem], tr.at[sem], at_v(k))

    t_cp = {k: t_copy(0, k, k) for k in (1, 7, 2, 6)}
    t_cp.update({3: t_copy(6, 1, 3), 5: t_copy(2, 7, 5), 4: t_copy(6, 2, 4)})
    for k in (1, 7, 2, 6):
        t_cp[k].start()
    w_cp = [remote(wbuf.at[y], wbuf.at[y], ws.at[k], wr.at[k], at_y(k)) for k in range(1, NY)]
    for cp in w_cp:
        cp.start()
    for cp in x1:
        cp.wait_recv()
    vo_cp.wait_recv()
    r64, c64 = iota((64, 64), 0), iota((64, 64), 1)
    perm2 = hot(c64 == (lax.rem(r64, 8) // 2) * 16 + (r64 // 8) * 2 + lax.rem(r64, 2))
    m0 = nn(perm2, mixb[0].reshape(64, VHD)).astype(BF)
    m1 = nn(perm2, mixb[1].reshape(64, VHD)).astype(BF)
    part = nn(m0, vo[0]) + nn(m1, vo[1])
    for k in range(NV):
        rs_src[k] = fold(part[8 * k : 8 * k + 8]).astype(BF)
    rs_cp = []
    for k in range(1, NV):
        cp = remote(rs_src.at[lax.rem(v + k, NV)], rs_buf.at[v], rss.at[k], rsr.at[k], at_v(k))
        cp.start()
        rs_cp.append(cp)
    rs_buf[v] = rs_src[v]
    t_cp[2].wait_recv()
    t_cp[6].wait_recv()
    for k in (3, 5, 4):
        t_cp[k].start()

    for load in loads[8:]:
        load.wait()
    r256, c256 = iota((256, 256), 0), iota((256, 256), 1)
    perm_w = hot(c256 == 2 * lax.rem(r256, 128) + r256 // 128)

    def split_w(i, z):
        both = nn(perm_w, wq_land[pl.ds(pl.multiple_of(i * 256, 256), 256), :]).astype(BF)
        at = pl.ds(pl.multiple_of(i * 128, 128), 128)
        wq[at, 0:128] = both[:128]
        wq[at, 128:256] = both[128:]
        return z

    lax.fori_loop(0, 32, split_w, 0)

    s_own = sorder[0, c]
    slices = (s_own, 2 * NC - 1 - s_own)
    ip = ipos[...]
    lane1024 = iota((1, 1024), 1)
    ishard = lane1024 // 32
    patches = jnp.sum(ipatch[...].astype(F32), axis=0, keepdims=True)
    eye32 = iota((32, 32), 0) == iota((32, 32), 1)
    pcol = jnp.sum(jnp.where(eye32, patches, 0.0), axis=1, keepdims=True)
    live_all = (ishard == iota((32, 1024), 0)) & ((4 * lax.rem(lane1024, 32)).astype(F32) < pcol)
    live = jnp.sum(jnp.where(live_all, 1.0, 0.0), axis=0, keepdims=True)
    ipf = ip.astype(F32)
    rows_col = iota((128, 1), 0)
    own_pos = jnp.where(rows_col < 64, slices[0] * 64, slices[1] * 64) + lax.rem(rows_col, 64)
    own_pos_f = own_pos.astype(F32)
    hit = jnp.where((own_pos == ip) & (live > 0.5), 1.0, 0.0)
    is_image = jnp.sum(hit, axis=1, keepdims=True) > 0.5
    gather32 = hot(iota((1024, 32), 0) // 32 == iota((1024, 32), 1))
    place = nn(hit.astype(BF), gather32).astype(BF)
    own_doc = jnp.zeros((128, 128), F32)
    for j in range(32):
        blk = docs[:, 128 * j : 128 * j + 128].astype(F32)
        own_doc = own_doc + jnp.where(own_pos == iota((1, 128), 1) + 128 * j, blk, 0.0)
    own_doc = jnp.sum(own_doc, axis=1, keepdims=True)
    below = jnp.zeros((128, 128), F32)
    for j in range(32):
        blk = docs[:, 128 * j : 128 * j + 128].astype(F32)
        below = below + jnp.where(blk < own_doc, 1.0, 0.0)
    low = jnp.sum(below, axis=1, keepdims=True)
    own_slot = lane1024 == c * 32 + iota((32, 1024), 0)
    own_ipos = jnp.sum(jnp.where(own_slot, ipf, 0.0), axis=1, keepdims=True)
    so_col = jnp.sum(jnp.where(eye32, sorder_v[...].astype(F32), 0.0), axis=1, keepdims=True)
    sl = ip // 64
    pair = jnp.minimum(sl, 2 * NC - 1 - sl).astype(F32)
    goes = hot((pair == so_col) & (ishard == c))
    in_off = hot(lax.rem(ip, 64) == iota((64, 1024), 0))
    low_half = nt(hot((sl.astype(F32) == so_col) & (live > 0.5)), in_off)
    high_half = nt(hot((sl.astype(F32) == 2 * NC - 1 - so_col) & (live > 0.5)), in_off)
    gone = jnp.concatenate([low_half, high_half], axis=1)
    offset = iota((1, 128), 1)
    shard_pos = jnp.where(offset < 64, so_col * 64, (2 * NC - 1 - so_col) * 64) + lax.rem(offset, 64).astype(F32)
    shard_pos = jnp.where(gone > 0.5, 1e9, shard_pos)
    for e in range(NC):
        kpos_s[e // 8, :, 128 * (e % 8) : 128 * (e % 8) + 128] = shard_pos[e : e + 1]
    ipos_live = jnp.where(live > 0.5, ipf, 1e9)
    gather32_t = hot(iota((32, 1024), 1) // 32 == iota((32, 1024), 0))
    place_t = nt(gather32_t, hit.astype(BF)) > 0.5
    low_row = jnp.sum(jnp.where(eye, low, 0.0), axis=0, keepdims=True)
    pos_row = jnp.sum(jnp.where(eye, own_pos_f, 0.0), axis=0, keepdims=True)
    low_i = jnp.sum(jnp.where(place_t, low_row, 0.0), axis=1, keepdims=True)
    pos_i = jnp.sum(jnp.where(place_t, pos_row, 0.0), axis=1, keepdims=True)
    fold32 = hot(lax.rem(iota((1024, 32), 0), 32) == iota((1024, 32), 1))
    select = nn(goes, fold32).astype(BF)
    cos_t, sin_t = angles_of(own_pos_f, freq[...])
    cos_i, sin_i = angles_of(own_ipos, freq[...])

    for cp in res_cp:
        cp.wait_recv()
    pick = hot(iota((8, 64), 1) == (iota((8, 64), 0) // 2) * 16 + 2 * v + lax.rem(iota((8, 64), 0), 2))
    residual = nn(pick, res[...].reshape(64, VD))
    for cp in rs_cp:
        cp.wait_recv()
    summed = rs_buf[0].astype(F32)
    for k in range(1, NV):
        summed = summed + rs_buf[k].astype(F32)
    hidden = residual + unfold(summed)
    merged8 = layer_norm(hidden, mgain[...].reshape(1, VD), mbias[...].reshape(1, VD))
    ag[t, v] = fold(merged8).astype(BF)
    ag_cp = [remote(ag.at[t, v], ag.at[t, v], ags.at[k], agr.at[k], at_v(k)) for k in range(1, NV)]
    for cp in ag_cp:
        cp.start()

    for k in (1, 7, 3, 5, 4):
        t_cp[k].wait_recv()
    t_fwd = remote(tbuf.at[t], tbuf.at[t], fs.at[0], fr.at[0], partner)
    t_fwd.start()
    t_fwd.wait_recv()

    def normalise(buf, dst, rows):
        def squares(i, total):
            blk = buf[lax.rem(i, 2), i // 2].astype(F32)
            return total + blk * blk

        total = lax.fori_loop(0, 16, squares, jnp.zeros((rows, 256), F32))
        scale = lax.rsqrt(jnp.sum(total, axis=1, keepdims=True) * (1.0 / D) + norm_eps)
        for i in range(16):
            cols = slice(256 * i, 256 * i + 256)
            dst[:, cols] = (buf[i % 2, i // 2].astype(F32) * scale * ngain[:, cols]).astype(BF)

    normalise(tbuf, ntext, TOK)
    kv_t = nn(ntext[...], wkv[...])
    kvbuf[t, c] = jnp.where(t == 0, rotate(kv_t, cos_t, sin_t), kv_t).astype(BF)

    def along(buf, ss, rs):
        def copy(n):
            blk = buf.at[t, x * NY + lax.rem(y + lax.rem(n, NY), NY)] if n >= NY else buf.at[t, c]
            d = at_x(n // NY, t) if n >= NY else at_y(n)
            return remote(blk, blk, ss.at[n], rs.at[n], d)

        return {n: copy(n) for n in range(1, NC)}

    def send_own(copies):
        for n in (1, 7, 2, 6, 3, 5, 4, 8, 24, 16):
            copies[n].start()

    def hand_on(copies, which):
        for k in which:
            copies[k].wait_recv()
            for dx in (1, 3, 2):
                copies[NY * dx + NY - k].start()

    kv_cp = along(kvbuf, kvs, kvr)
    send_own(kv_cp)

    for cp in ag_cp:
        cp.wait_recv()
    ag_fwd = remote(ag.at[t], ag.at[t], fs.at[1], fr.at[1], partner)
    ag_fwd.start()
    for cp in w_cp:
        cp.wait_recv()
    ag_fwd.wait_recv()
    half_of, rest = r256 // 128, lax.rem(r256, 128)
    xs, j = rest // 32, lax.rem(rest, 32)
    perm3 = hot(c256 == (j // 16) * 128 + (lax.rem(j, 16) // 2) * 16 + half_of * 8 + xs * 2 + lax.rem(j, 2))
    mp = nn(perm3, ag[...].reshape(256, 640)).astype(BF)
    wg = wbuf[...].reshape(VD, 256)
    yv = nn(mp[:128], wg[:640]) + nn(mp[128:], wg[640:])
    ysrc[...] = yv.reshape(NX, 32, 256)
    y_cp = []
    for k in range(1, NX):
        cp = remote(ysrc.at[lax.rem(x + k, NX)], ybuf.at[x], ys.at[k], yr.at[k], at_x(k, t))
        cp.start()
        y_cp.append(cp)
    ybuf[x] = ysrc[x]

    hand_on(kv_cp, (1, 7, 2, 6))
    for cp in y_cp:
        cp.wait_recv()
    emb = ybuf[0]
    for k in range(1, NX):
        emb = emb + ybuf[k]
    p4[t, v] = emb.astype(BF)
    p4_cp = [remote(p4.at[t, v], p4.at[t, v], p4s.at[k], p4r.at[k], at_v(k)) for k in range(1, NV)]
    for cp in p4_cp:
        cp.start()
    hand_on(kv_cp, (3, 5, 4))
    q_t = nn(ntext[...], wq[...])
    q_t = [rotate(q_t[:, :128], cos_t, sin_t).astype(BF), rotate(q_t[:, 128:], cos_t, sin_t).astype(BF)]

    for cp in p4_cp:
        cp.wait_recv()
    p4_fwd = remote(p4.at[t], p4.at[t], fs.at[2], fr.at[2], partner)
    p4_fwd.start()
    p4_fwd.wait_recv()
    normalise(p4, nimg, 32)
    kv_i = nn(nimg[...], wkv[...])
    kibuf[t, c] = jnp.where(t == 0, rotate(kv_i, cos_i, sin_i), kv_i).astype(BF)
    ki_cp = along(kibuf, kis, kir)
    send_own(ki_cp)
    q_i = nn(nimg[...], wq[...])
    q_i = jnp.concatenate(
        [rotate(q_i[:, :128], cos_i, sin_i), rotate(q_i[:, 128:], cos_i, sin_i)], axis=1
    ).astype(BF)
    q_go = nn(select, q_i)
    for e in range(NC):
        qsrc[e] = q_go[e : e + 1]
    qbuf[c] = qsrc[c]

    def q_copy(k):
        return remote(qsrc.at[lax.rem(c + k, NC)], qbuf.at[c], qs.at[k], qr.at[k], at_c(k))

    lax.fori_loop(1, NC, lambda k, z: (q_copy(k).start(), z)[1], 0)
    hand_on(ki_cp, (1, 7, 2, 6, 3, 5, 4))

    for n in range(NY, NC):
        kv_cp[n].wait_recv()
    kv_fwd = remote(kvbuf.at[t], kvbuf.at[t], fs.at[3], fr.at[3], partner)
    kv_fwd.start()
    kv_fwd.wait_recv()
    scale = 1.0 / math.sqrt(HD)

    def attend(state, queries, qpos, qlow, keys, values, kpos):
        best, total, acc = state
        sc = nt(queries, keys) * scale
        sc = jnp.where((kpos >= qlow) & (kpos <= qpos), sc, big_negative)
        new = jnp.maximum(best, jnp.max(sc, axis=1, keepdims=True))
        factor = jnp.exp(best - new)
        p = jnp.exp(sc - new)
        total = total * factor + jnp.sum(p, axis=1, keepdims=True)
        return new, total, acc * factor + nn(p.astype(BF), values)

    def over_text(queries, qpos, qlow):
        rows = queries.shape[0]
        state = (jnp.full((rows, 1), big_negative, F32), jnp.zeros((rows, 1), F32), jnp.zeros((rows, HD), F32))

        def block(b, state):
            at = pl.ds(b * 8, 8)
            keys = kvbuf[0, at].reshape(1024, HD)
            values = kvbuf[1, at].reshape(1024, HD)
            return attend(state, queries, qpos, qlow, keys, values, kpos_s[b])

        return lax.fori_loop(0, 4, block, state)

    queries_t = jnp.concatenate(q_t, axis=0)
    pos2, low2 = jnp.concatenate([own_pos_f] * 2, axis=0), jnp.concatenate([low] * 2, axis=0)
    state_t = over_text(queries_t, pos2, low2)

    for n in range(NY, NC):
        ki_cp[n].wait_recv()
    ki_fwd = remote(kibuf.at[t], kibuf.at[t], fs.at[4], fr.at[4], partner)
    ki_fwd.start()
    lax.fori_loop(1, NC, lambda k, z: (q_copy(k).wait_recv(), z)[1], 0)
    q_in = jnp.concatenate([qbuf[e] for e in range(NC)], axis=0).astype(BF)
    queries_i = jnp.concatenate([q_in[:, :128], q_in[:, 128:]], axis=0)
    pos2_i, low2_i = jnp.concatenate([pos_i] * 2, axis=0), jnp.concatenate([low_i] * 2, axis=0)
    state_i = over_text(queries_i, pos2_i, low2_i)
    ki_fwd.wait_recv()
    state = attend(
        [jnp.concatenate(parts, axis=0) for parts in zip(state_t, state_i, strict=True)],
        jnp.concatenate([queries_t, queries_i], axis=0),
        jnp.concatenate([pos2, pos2_i], axis=0),
        jnp.concatenate([low2, low2_i], axis=0),
        kibuf[0].reshape(1024, HD),
        kibuf[1].reshape(1024, HD),
        ipos_live,
    )
    result = (state[2] / state[1]).astype(BF)
    for g in range(2):
        placed = nn(place, result[256 + 32 * g : 288 + 32 * g])
        mixed = jnp.where(is_image, placed, result[128 * g : 128 * g + 128].astype(F32))
        out[:, 128 * g : 128 * g + 128] = mixed.astype(BF)

    for cp in x1 + [vo_cp] + res_cp + w_cp + list(t_cp.values()) + rs_cp + ag_cp + y_cp + p4_cp:
        cp.wait_send()
    for cp in (t_fwd, ag_fwd, p4_fwd, kv_fwd, ki_fwd):
        cp.wait_send()
    for n in range(1, NC):
        kv_cp[n].wait_send()
        ki_cp[n].wait_send()
    lax.fori_loop(1, NC, lambda k, z: (q_copy(k).wait_send(), z)[1], 0)


def local(
    patch_rows, vit_gain, vit_bias, vit_qkv, vit_out, merge_gain, merge_bias, merge_weight,
    image_patches, window_ids, image_pos, slice_order, doc_ids, text_rows, norm_gain, w_query, w_keyval,
):
    exponent = np.arange(64, dtype=np.float64) * (-2.0 / HD)
    freq = np.power(np.float64(rope_base), exponent).astype(np.float32)
    freq = jnp.asarray(np.concatenate([freq, freq])[None, :])
    vm = pl.BlockSpec(memory_space=pltpu.VMEM)
    dma = pltpu.SemaphoreType.DMA
    args = [
        patch_rows,
        vit_gain,
        vit_bias,
        jnp.transpose(vit_qkv, (1, 2, 3, 0)).reshape(3 * VHD, VD),
        vit_out.reshape(VHD, VD),
        merge_gain,
        merge_bias,
        merge_weight,
        jnp.transpose(image_patches),
        window_ids.reshape(1, 128),
        image_pos.reshape(1, 1024),
        slice_order.reshape(1, NC),
        doc_ids.reshape(1, 4096),
        text_rows,
        norm_gain.reshape(1, D),
        w_query.reshape(2 * D, HD),
        w_keyval.reshape(D, HD),
        freq,
    ]
    scratch = [
        pltpu.VMEM((128, VD), BF),
        pltpu.VMEM((VD,), F32),
        pltpu.VMEM((VD,), F32),
        pltpu.VMEM((3 * VHD, VD), BF),
        pltpu.VMEM((VD,), F32),
        pltpu.VMEM((VD,), F32),
        pltpu.VMEM((2, NC), jnp.int32),
        pltpu.VMEM((1, 128), jnp.int32),
        pltpu.VMEM((1, 1024), jnp.int32),
        pltpu.SMEM((1, NC), jnp.int32),
        pltpu.VMEM((1, NC), jnp.int32),
        pltpu.VMEM((1, 4096), jnp.int32),
        pltpu.VMEM((1, D), F32),
        pltpu.VMEM((1, HD), F32),
        pltpu.VMEM((2 * D, HD), BF),
        pltpu.VMEM((D, 2 * HD), BF),
        pltpu.VMEM((D, HD), BF),
        pltpu.VMEM((NY, 160, 256), BF),
        pltpu.VMEM((NT, NV, TOK, 256), BF),
        pltpu.VMEM((TOK, D), BF),
        pltpu.VMEM((NT, NC, TOK, HD), BF),
        pltpu.VMEM((NT, NC, 32, HD), BF),
        pltpu.VMEM((8, 16, VHD), BF),
        pltpu.VMEM((NT, NX, 16, VHD), BF),
        pltpu.VMEM((NT, VHD, VD), BF),
        pltpu.VMEM((8, 16, VD), BF),
        pltpu.VMEM((NX, 16, VD), BF),
        pltpu.VMEM((NV, 16, 640), BF),
        pltpu.VMEM((NV, 16, 640), BF),
        pltpu.VMEM((NT, NV, 16, 640), BF),
        pltpu.VMEM((NX, 32, 256), F32),
        pltpu.VMEM((NX, 32, 256), F32),
        pltpu.VMEM((NT, NV, 32, 256), BF),
        pltpu.VMEM((32, D), BF),
        pltpu.VMEM((NC, 1, 256), F32),
        pltpu.VMEM((NC, 1, 256), F32),
        pltpu.VMEM((4, 1, 1024), F32),
        dma((19,)),
        dma((8,)), dma((8,)),
        dma, dma,
        dma((NX,)), dma((NX,)),
        dma((NY,)), dma((NY,)),
        dma((NV,)), dma((NV,)),
        dma((NV,)), dma((NV,)),
        dma((NV,)), dma((NV,)),
        dma((NX,)), dma((NX,)),
        dma((NV,)), dma((NV,)),
        dma((NC,)), dma((NC,)),
        dma((NC,)), dma((NC,)),
        dma((NC,)), dma((NC,)),
        dma((5,)), dma((5,)),
    ]
    result = pl.pallas_call(
        kernel,
        name="fused",
        out_shape=jax.ShapeDtypeStruct((TOK, 256), BF),
        in_specs=[pl.BlockSpec(memory_space=pl.ANY)] * len(args),
        out_specs=vm,
        scratch_shapes=scratch,
        compiler_params=pltpu.CompilerParams(
            collective_id=0, has_side_effects=True, vmem_limit_bytes=63 << 20
        ),
    )(*args)
    return result.reshape(TOK, 1, 256)


def solution(mesh):
    placed = (
        P("ctx", None),
        P(),
        P(),
        P(None, None, ("vis", "tp"), None),
        P(("vis", "tp"), None, None),
        P(),
        P(),
        P("ctx", ("vis", "tp")),
        P(),
        P("ctx"),
        P(),
        P(),
        P(),
        P("ctx", ("vis", "tp")),
        P(),
        P(None, "vis", "tp", None),
        P("tp", None, "vis", None),
    )
    return jax.shard_map(
        local, mesh=mesh, in_specs=placed, out_specs=P("ctx", "vis", "tp"), check_vma=False
    )
```

```python
import functools
import math

import jax
import jax.numpy as jnp
import numpy as np
from jax import lax
from jax.experimental import pallas as pl
from jax.experimental.pallas import tpu as pltpu
from jax.sharding import PartitionSpec as P

D = 4096
HD = 128
VD = 1280
VHD = 80
TOK = 128
NV, NX, NY, NT = 8, 4, 8, 2
NC = NX * NY

norm_eps = 1e-06
rope_base = 1000000.0
big_negative = -1e30
MESH = pl.DeviceIdType.MESH
F32 = jnp.float32
BF = jnp.bfloat16


def nn(a, b):
    return lax.dot_general(a, b, (((1,), (0,)), ((), ())), preferred_element_type=F32)


def nt(a, b):
    return lax.dot_general(a, b, (((1,), (1,)), ((), ())), preferred_element_type=F32)


def iota(shape, dim):
    return lax.broadcasted_iota(jnp.int32, shape, dim)


def hot(mask):
    return jnp.where(mask, 1.0, 0.0).astype(BF)


def layer_norm(values, scale_vec, shift_vec):
    centre = jnp.mean(values, axis=-1, keepdims=True)
    offset = values - centre
    spread = jnp.mean(offset * offset, axis=-1, keepdims=True)
    return offset * lax.rsqrt(spread + norm_eps) * scale_vec + shift_vec


def rotate(values, cosine, sine):
    return values * cosine + pltpu.roll(values, 64, 1) * sine


def angles_of(pos_column, freq_row):
    ang = pos_column * freq_row
    sign = jnp.where(iota(ang.shape, 1) < 64, -1.0, 1.0)
    return jnp.cos(ang), jnp.sin(ang) * sign


def fold(rows8):
    return jnp.concatenate([rows8[:, :640], rows8[:, 640:]], axis=0)


def unfold(rows16):
    return jnp.concatenate([rows16[:8], rows16[8:]], axis=1)


def kernel(
    patch_h, vgain_h, vbias_h, wqkv_h, vout, mgain_h, mbias_h, wblk, ipatch_h, wids_h, ipos_h, sorder_h, docs_h,
    text, ngain_h, wq_raw, wkv_in, freq_h, out,
    patch, vgain, vbias, wqkv, mgain, mbias, ipatch, wids, ipos, sorder, sorder_v, docs, ngain, freq,
    wq_land, wq, wkv, wbuf, tbuf, ntext, kvbuf, kibuf, blp, mixb, vo, pp, res,
    rs_src, rs_buf, ag, ysrc, ybuf, p4, nimg, n16, qsrc, qbuf, kpos_s,
    lsem, x1s, x1r, vos, vor, ress, resr, ws, wr, ts, tr, rss, rsr, ags, agr, ys, yr,
    p4s, p4r, kvs, kvr, kis, kir, qs, qr, fs, fr, tfs, tfr,
):
    v, c, t = lax.axis_index("vis"), lax.axis_index("ctx"), lax.axis_index("tp")
    x, y = c // NY, lax.rem(c, NY)
    other = 1 - t

    def at_v(k):
        return (lax.rem(v + k, NV), c, t)

    def at_c(k):
        return (v, lax.rem(c + k, NC), t)

    def at_y(k):
        return (v, x * NY + lax.rem(y + k, NY), t)

    def at_x(k, tt):
        return (v, lax.rem(x + k, NX) * NY + y, tt)

    partner = (v, c, other)

    pairs = [
        (patch_h, patch), (vgain_h, vgain), (vbias_h, vbias), (wqkv_h, wqkv), (wids_h, wids),
        (vout, vo.at[t]), (text, tbuf.at[t, v]), (wblk, wbuf.at[t, y]),
        (wq_raw, wq_land), (mgain_h, mgain), (mbias_h, mbias), (ipatch_h, ipatch), (ipos_h, ipos),
        (sorder_h, sorder_v), (sorder_h, sorder), (docs_h, docs), (ngain_h, ngain), (freq_h, freq), (wkv_in, wkv),
    ]
    loads = [pltpu.make_async_copy(a, b, lsem.at[n]) for n, (a, b) in enumerate(pairs)]
    for load in loads[:5]:
        load.start()

    barrier = pltpu.get_barrier_semaphore()

    def greet(d):
        pl.semaphore_signal(barrier, inc=1, device_id=d, device_id_type=MESH)

    lax.fori_loop(1, NV, lambda k, z: (greet(at_v(k)), z)[1], 0)
    lax.fori_loop(1, NC, lambda k, z: (greet(at_c(k)), z)[1], 0)
    for k in range(1, NX):
        greet(at_x(k, other))
    greet(partner)
    greetings = (NV - 1) + (NC - 1) + (NX - 1) + 1
    for load in loads[5:]:
        load.start()


    def remote(src, dst, ssem, rsem, d):
        return pltpu.make_async_remote_copy(
            src_ref=src, dst_ref=dst, send_sem=ssem, recv_sem=rsem, device_id=d, device_id_type=MESH
        )

    for load in loads[:5]:
        load.wait()
    normed = layer_norm(patch[...].astype(F32), vgain[...].reshape(1, VD), vbias[...].reshape(1, VD)).astype(BF)
    vq = nt(normed, wqkv[0:80, :]).astype(BF)
    vk = nt(normed, wqkv[80:160, :]).astype(BF)
    vv = nt(normed, wqkv[160:240, :]).astype(BF)
    wrow = wids[...]
    eye = iota((128, 128), 0) == iota((128, 128), 1)
    wcol = jnp.sum(jnp.where(eye, wrow, 0).astype(F32), axis=1, keepdims=True)
    scores = nt(vq, vk) / math.sqrt(VHD)
    scores = jnp.where(wcol == wrow.astype(F32), scores, big_negative)
    powers = jnp.exp(scores - jnp.max(scores, axis=-1, keepdims=True))
    totals = jnp.sum(powers, axis=-1, keepdims=True)
    blended = (nn(powers.astype(BF), vv) / totals).astype(BF)
    perm1 = hot(iota((128, 128), 1) == 4 * lax.rem(iota((128, 128), 0), 32) + iota((128, 128), 0) // 32)
    blp[...] = nn(perm1, blended).astype(BF).reshape(8, 16, VHD)
    pp[...] = nn(perm1, patch[...]).astype(BF).reshape(8, 16, VD)
    mixb[t, x] = blp[x * 2 + t]
    res[x] = pp[x * 2 + t]

    pl.semaphore_wait(barrier, greetings)

    x1 = []
    for k in range(NX):
        for dt in range(NT):
            if k + dt:
                tt = t if dt == 0 else other
                xx = lax.rem(x + k, NX)
                n = k * 2 + dt
                x1.append(remote(blp.at[xx * 2 + tt], mixb.at[t, x], x1s.at[n], x1r.at[n], at_x(k, tt)))
    for cp in x1:
        cp.start()
    for load in loads[5:8]:
        load.wait()
    vo_cp = remote(vo.at[t], vo.at[t], vos, vor, partner)
    vo_cp.start()
    res_cp = []
    for k in range(1, NX):
        res_cp.append(remote(pp.at[lax.rem(x + k, NX) * 2 + t], res.at[x], ress.at[k], resr.at[k], at_x(k, t)))
        res_cp[-1].start()
    def t_copy(block, k, sem):
        blk = tbuf.at[t, lax.rem(v + block, NV)]
        return remote(blk, blk, ts.at[sem], tr.at[sem], at_v(k))

    t_cp = {k: t_copy(0, k, k) for k in (1, 7, 2, 6)}
    t_cp.update({3: t_copy(6, 1, 3), 5: t_copy(2, 7, 5), 4: t_copy(6, 2, 4)})
    for k in (1, 7, 2, 6):
        t_cp[k].start()
    w_cp = [remote(wbuf.at[t, y], wbuf.at[t, y], ws.at[k], wr.at[k], at_y(k)) for k in range(1, NY)]
    for cp in w_cp:
        cp.start()
    for cp in x1:
        cp.wait_recv()
    vo_cp.wait_recv()
    r64, c64 = iota((64, 64), 0), iota((64, 64), 1)
    perm2 = hot(c64 == (lax.rem(r64, 8) // 2) * 16 + (r64 // 8) * 2 + lax.rem(r64, 2))
    m0 = nn(perm2, mixb[0].reshape(64, VHD)).astype(BF)
    m1 = nn(perm2, mixb[1].reshape(64, VHD)).astype(BF)
    part = nn(m0, vo[0]) + nn(m1, vo[1])
    for k in range(NV):
        rs_src[k] = fold(part[8 * k : 8 * k + 8]).astype(BF)
    rs_cp = []
    for k in range(1, NV):
        cp = remote(rs_src.at[lax.rem(v + k, NV)], rs_buf.at[v], rss.at[k], rsr.at[k], at_v(k))
        cp.start()
        rs_cp.append(cp)
    rs_buf[v] = rs_src[v]
    t_cp[2].wait_recv()
    t_cp[6].wait_recv()
    for k in (3, 5, 4):
        t_cp[k].start()

    def t_other(k):
        blk = tbuf.at[t, lax.rem(v + k, NV)]
        return remote(blk, blk, tfs.at[k], tfr.at[k], partner)

    t_fwd = [t_other(k) for k in range(NV)]
    t_cp[1].wait_recv()
    t_cp[7].wait_recv()
    for k in (0, 1, 7, 2, 6):
        t_fwd[k].start()

    for load in loads[8:]:
        load.wait()
    r256, c256 = iota((256, 256), 0), iota((256, 256), 1)
    perm_w = hot(c256 == 2 * lax.rem(r256, 128) + r256 // 128)

    def split_w(i, z):
        both = nn(perm_w, wq_land[pl.ds(pl.multiple_of(i * 256, 256), 256), :]).astype(BF)
        at = pl.ds(pl.multiple_of(i * 128, 128), 128)
        wq[at, 0:128] = both[:128]
        wq[at, 128:256] = both[128:]
        return z

    lax.fori_loop(0, 32, split_w, 0)

    s_own = sorder[0, c]
    slices = (s_own, 2 * NC - 1 - s_own)
    ip = ipos[...]
    lane1024 = iota((1, 1024), 1)
    ishard = lane1024 // 32
    patches = jnp.sum(ipatch[...].astype(F32), axis=0, keepdims=True)
    eye32 = iota((32, 32), 0) == iota((32, 32), 1)
    pcol = jnp.sum(jnp.where(eye32, patches, 0.0), axis=1, keepdims=True)
    live_all = (ishard == iota((32, 1024), 0)) & ((4 * lax.rem(lane1024, 32)).astype(F32) < pcol)
    live = jnp.sum(jnp.where(live_all, 1.0, 0.0), axis=0, keepdims=True)
    ipf = ip.astype(F32)
    rows_col = iota((128, 1), 0)
    own_pos = jnp.where(rows_col < 64, slices[0] * 64, slices[1] * 64) + lax.rem(rows_col, 64)
    own_pos_f = own_pos.astype(F32)
    hit = jnp.where((own_pos == ip) & (live > 0.5), 1.0, 0.0)
    is_image = jnp.sum(hit, axis=1, keepdims=True) > 0.5
    gather32 = hot(iota((1024, 32), 0) // 32 == iota((1024, 32), 1))
    place = nn(hit.astype(BF), gather32).astype(BF)
    own_doc = jnp.zeros((128, 128), F32)
    for j in range(32):
        blk = docs[:, 128 * j : 128 * j + 128].astype(F32)
        own_doc = own_doc + jnp.where(own_pos == iota((1, 128), 1) + 128 * j, blk, 0.0)
    own_doc = jnp.sum(own_doc, axis=1, keepdims=True)
    below = jnp.zeros((128, 128), F32)
    for j in range(32):
        blk = docs[:, 128 * j : 128 * j + 128].astype(F32)
        below = below + jnp.where(blk < own_doc, 1.0, 0.0)
    low = jnp.sum(below, axis=1, keepdims=True)
    own_slot = lane1024 == c * 32 + iota((32, 1024), 0)
    own_ipos = jnp.sum(jnp.where(own_slot, ipf, 0.0), axis=1, keepdims=True)
    so_col = jnp.sum(jnp.where(eye32, sorder_v[...].astype(F32), 0.0), axis=1, keepdims=True)
    sl = ip // 64
    pair = jnp.minimum(sl, 2 * NC - 1 - sl).astype(F32)
    goes = hot((pair == so_col) & (ishard == c))
    in_off = hot(lax.rem(ip, 64) == iota((64, 1024), 0))
    low_half = nt(hot((sl.astype(F32) == so_col) & (live > 0.5)), in_off)
    high_half = nt(hot((sl.astype(F32) == 2 * NC - 1 - so_col) & (live > 0.5)), in_off)
    gone = jnp.concatenate([low_half, high_half], axis=1)
    offset = iota((1, 128), 1)
    shard_pos = jnp.where(offset < 64, so_col * 64, (2 * NC - 1 - so_col) * 64) + lax.rem(offset, 64).astype(F32)
    shard_pos = jnp.where(gone > 0.5, 1e9, shard_pos)
    for e in range(NC):
        kpos_s[e // 8, :, 128 * (e % 8) : 128 * (e % 8) + 128] = shard_pos[e : e + 1]
    ipos_live = jnp.where(live > 0.5, ipf, 1e9)
    gather32_t = hot(iota((32, 1024), 1) // 32 == iota((32, 1024), 0))
    place_t = nt(gather32_t, hit.astype(BF)) > 0.5
    low_row = jnp.sum(jnp.where(eye, low, 0.0), axis=0, keepdims=True)
    pos_row = jnp.sum(jnp.where(eye, own_pos_f, 0.0), axis=0, keepdims=True)
    low_i = jnp.sum(jnp.where(place_t, low_row, 0.0), axis=1, keepdims=True)
    pos_i = jnp.sum(jnp.where(place_t, pos_row, 0.0), axis=1, keepdims=True)
    fold32 = hot(lax.rem(iota((1024, 32), 0), 32) == iota((1024, 32), 1))
    select = nn(goes, fold32).astype(BF)
    cos_t, sin_t = angles_of(own_pos_f, freq[...])
    cos_i, sin_i = angles_of(own_ipos, freq[...])

    for cp in res_cp:
        cp.wait_recv()
    pick = hot(iota((8, 64), 1) == (iota((8, 64), 0) // 2) * 16 + 2 * v + lax.rem(iota((8, 64), 0), 2))
    residual = nn(pick, res[...].reshape(64, VD))
    for cp in rs_cp:
        cp.wait_recv()
    summed = rs_buf[0].astype(F32)
    for k in range(1, NV):
        summed = summed + rs_buf[k].astype(F32)
    hidden = residual + unfold(summed)
    merged8 = layer_norm(hidden, mgain[...].reshape(1, VD), mbias[...].reshape(1, VD))
    ag[v] = fold(merged8).astype(BF)
    ag_cp = [remote(ag.at[v], ag.at[v], ags.at[k], agr.at[k], at_v(k)) for k in range(1, NV)]
    for cp in ag_cp:
        cp.start()

    for cp in w_cp:
        cp.wait_recv()
    w_fwd = remote(wbuf.at[t], wbuf.at[t], fs.at[1], fr.at[1], partner)
    w_fwd.start()

    for k in (3, 5, 4):
        t_cp[k].wait_recv()
        t_fwd[NV - k].start()
    for k in range(NV):
        t_fwd[k].wait_recv()

    def normalise(buf, dst, rows):
        def squares(i, total):
            blk = buf(lax.rem(i, 2), i // 2).astype(F32)
            return total + blk * blk

        total = lax.fori_loop(0, 16, squares, jnp.zeros((rows, 256), F32))
        scale = lax.rsqrt(jnp.sum(total, axis=1, keepdims=True) * (1.0 / D) + norm_eps)
        for i in range(16):
            cols = slice(256 * i, 256 * i + 256)
            dst[:, cols] = (buf(i % 2, i // 2).astype(F32) * scale * ngain[:, cols]).astype(BF)

    normalise(lambda a, b: tbuf[a, b], ntext, TOK)
    kv_t = nn(ntext[...], wkv[...])
    kvbuf[t, c] = jnp.where(t == 0, rotate(kv_t, cos_t, sin_t), kv_t).astype(BF)

    def along(buf, ss, rs):
        def copy(n):
            blk = buf.at[t, x * NY + lax.rem(y + lax.rem(n, NY), NY)] if n >= NY else buf.at[t, c]
            d = at_x(n // NY, t) if n >= NY else at_y(n)
            return remote(blk, blk, ss.at[n], rs.at[n], d)

        return {n: copy(n) for n in range(1, NC)}

    def send_own(copies):
        for n in (1, 7, 2, 6, 3, 5, 4, 8, 24, 16):
            copies[n].start()

    def hand_on(copies, which):
        for k in which:
            copies[k].wait_recv()
            for dx in (1, 3, 2):
                copies[NY * dx + NY - k].start()

    kv_cp = along(kvbuf, kvs, kvr)
    send_own(kv_cp)

    for cp in ag_cp:
        cp.wait_recv()
    w_fwd.wait_recv()
    r128, c128 = iota((128, 128), 0), iota((128, 128), 1)
    half_of, xs, j = r128 // 64, lax.rem(r128, 64) // 16, lax.rem(r128, 16)
    perm3 = hot(c128 == (j // 2) * 16 + half_of * 8 + xs * 2 + lax.rem(j, 2))
    mp = nn(perm3, ag[...].reshape(128, 640)).astype(BF)
    for tt in range(NT):
        wg = wbuf[tt].reshape(VD, 256)
        yv = nn(mp[:64], wg[:640]) + nn(mp[64:], wg[640:])
        ysrc[:, tt] = yv.reshape(NX, 16, 256)
    y_cp = []
    for k in range(1, NX):
        cp = remote(ysrc.at[lax.rem(x + k, NX)], ybuf.at[x], ys.at[k], yr.at[k], at_x(k, t))
        cp.start()
        y_cp.append(cp)
    ybuf[x] = ysrc[x]

    hand_on(kv_cp, (1, 7, 2, 6))
    for cp in y_cp:
        cp.wait_recv()
    emb = ybuf[0]
    for k in range(1, NX):
        emb = emb + ybuf[k]
    p4[v] = emb.astype(BF)
    p4_cp = [remote(p4.at[v], p4.at[v], p4s.at[k], p4r.at[k], at_v(k)) for k in range(1, NV)]
    for cp in p4_cp:
        cp.start()
    hand_on(kv_cp, (3, 5, 4))
    q_t = nn(ntext[...], wq[...])
    q_t = [rotate(q_t[:, :128], cos_t, sin_t).astype(BF), rotate(q_t[:, 128:], cos_t, sin_t).astype(BF)]

    for cp in p4_cp:
        cp.wait_recv()
    own_rows = pl.ds(pl.multiple_of(16 * t, 16), 16)
    normalise(lambda a, b: p4[b, a], n16, 16)
    nimg[own_rows, :] = n16[...]
    p4_fwd = remote(n16, nimg.at[own_rows, :], fs.at[2], fr.at[2], partner)
    p4_fwd.start()
    p4_fwd.wait_recv()
    kv_i = nn(nimg[...], wkv[...])
    kibuf[t, c] = jnp.where(t == 0, rotate(kv_i, cos_i, sin_i), kv_i).astype(BF)
    ki_cp = along(kibuf, kis, kir)
    send_own(ki_cp)
    q_i = nn(nimg[...], wq[...])
    q_i = jnp.concatenate(
        [rotate(q_i[:, :128], cos_i, sin_i), rotate(q_i[:, 128:], cos_i, sin_i)], axis=1
    ).astype(BF)
    q_go = nn(select, q_i)
    for e in range(NC):
        qsrc[e] = q_go[e : e + 1]
    qbuf[c] = qsrc[c]

    def q_copy(k):
        return remote(qsrc.at[lax.rem(c + k, NC)], qbuf.at[c], qs.at[k], qr.at[k], at_c(k))

    lax.fori_loop(1, NC, lambda k, z: (q_copy(k).start(), z)[1], 0)
    for n in range(NY, NC):
        kv_cp[n].wait_recv()
    kv_fwd = remote(kvbuf.at[t], kvbuf.at[t], fs.at[3], fr.at[3], partner)
    kv_fwd.start()
    hand_on(ki_cp, (1, 7, 2, 6))
    kv_fwd.wait_recv()
    scale = 1.0 / math.sqrt(HD)

    def attend(state, queries, qpos, qlow, keys, values, kpos):
        best, total, acc = state
        sc = nt(queries, keys) * scale
        sc = jnp.where((kpos >= qlow) & (kpos <= qpos), sc, big_negative)
        new = jnp.maximum(best, jnp.max(sc, axis=1, keepdims=True))
        factor = jnp.exp(best - new)
        p = jnp.exp(sc - new)
        total = total * factor + jnp.sum(p, axis=1, keepdims=True)
        return new, total, acc * factor + nn(p.astype(BF), values)

    def empty(rows):
        return jnp.full((rows, 1), big_negative, F32), jnp.zeros((rows, 1), F32), jnp.zeros((rows, HD), F32)

    def over_text(state, queries, qpos, qlow, blocks):
        def block(b, state):
            at = pl.ds(b * 8, 8)
            keys = kvbuf[0, at].reshape(1024, HD)
            values = kvbuf[1, at].reshape(1024, HD)
            return attend(state, queries, qpos, qlow, keys, values, kpos_s[b])

        return lax.fori_loop(*blocks, block, state)

    queries_t = jnp.concatenate(q_t, axis=0)
    pos2, low2 = jnp.concatenate([own_pos_f] * 2, axis=0), jnp.concatenate([low] * 2, axis=0)
    state_t = over_text(empty(256), queries_t, pos2, low2, (0, 2))
    hand_on(ki_cp, (3, 5, 4))
    state_t = over_text(state_t, queries_t, pos2, low2, (2, 4))

    for n in range(NY, NC):
        ki_cp[n].wait_recv()
    ki_fwd = remote(kibuf.at[t], kibuf.at[t], fs.at[4], fr.at[4], partner)
    ki_fwd.start()
    lax.fori_loop(1, NC, lambda k, z: (q_copy(k).wait_recv(), z)[1], 0)
    q_in = jnp.concatenate([qbuf[e] for e in range(NC)], axis=0).astype(BF)
    queries_i = jnp.concatenate([q_in[:, :128], q_in[:, 128:]], axis=0)
    pos2_i, low2_i = jnp.concatenate([pos_i] * 2, axis=0), jnp.concatenate([low_i] * 2, axis=0)
    state_i = over_text(empty(64), queries_i, pos2_i, low2_i, (0, 4))
    ki_fwd.wait_recv()
    state = attend(
        [jnp.concatenate(parts, axis=0) for parts in zip(state_t, state_i, strict=True)],
        jnp.concatenate([queries_t, queries_i], axis=0),
        jnp.concatenate([pos2, pos2_i], axis=0),
        jnp.concatenate([low2, low2_i], axis=0),
        kibuf[0].reshape(1024, HD),
        kibuf[1].reshape(1024, HD),
        ipos_live,
    )
    result = (state[2] / state[1]).astype(BF)
    for g in range(2):
        placed = nn(place, result[256 + 32 * g : 288 + 32 * g])
        mixed = jnp.where(is_image, placed, result[128 * g : 128 * g + 128].astype(F32))
        out[:, 128 * g : 128 * g + 128] = mixed.astype(BF)

    for cp in x1 + [vo_cp] + res_cp + w_cp + list(t_cp.values()) + rs_cp + ag_cp + y_cp + p4_cp:
        cp.wait_send()
    for cp in t_fwd + [w_fwd, p4_fwd, kv_fwd, ki_fwd]:
        cp.wait_send()
    for n in range(1, NC):
        kv_cp[n].wait_send()
        ki_cp[n].wait_send()
    lax.fori_loop(1, NC, lambda k, z: (q_copy(k).wait_send(), z)[1], 0)


def local(
    patch_rows, vit_gain, vit_bias, vit_qkv, vit_out, merge_gain, merge_bias, merge_weight,
    image_patches, window_ids, image_pos, slice_order, doc_ids, text_rows, norm_gain, w_query, w_keyval,
):
    exponent = np.arange(64, dtype=np.float64) * (-2.0 / HD)
    freq = np.power(np.float64(rope_base), exponent).astype(np.float32)
    freq = jnp.asarray(np.concatenate([freq, freq])[None, :])
    vm = pl.BlockSpec(memory_space=pltpu.VMEM)
    dma = pltpu.SemaphoreType.DMA
    args = [
        patch_rows,
        vit_gain,
        vit_bias,
        jnp.transpose(vit_qkv, (1, 2, 3, 0)).reshape(3 * VHD, VD),
        vit_out.reshape(VHD, VD),
        merge_gain,
        merge_bias,
        merge_weight,
        jnp.transpose(image_patches),
        window_ids.reshape(1, 128),
        image_pos.reshape(1, 1024),
        slice_order.reshape(1, NC),
        doc_ids.reshape(1, 4096),
        text_rows,
        norm_gain.reshape(1, D),
        w_query.reshape(2 * D, HD),
        w_keyval.reshape(D, HD),
        freq,
    ]
    scratch = [
        pltpu.VMEM((128, VD), BF),
        pltpu.VMEM((VD,), F32),
        pltpu.VMEM((VD,), F32),
        pltpu.VMEM((3 * VHD, VD), BF),
        pltpu.VMEM((VD,), F32),
        pltpu.VMEM((VD,), F32),
        pltpu.VMEM((2, NC), jnp.int32),
        pltpu.VMEM((1, 128), jnp.int32),
        pltpu.VMEM((1, 1024), jnp.int32),
        pltpu.SMEM((1, NC), jnp.int32),
        pltpu.VMEM((1, NC), jnp.int32),
        pltpu.VMEM((1, 4096), jnp.int32),
        pltpu.VMEM((1, D), F32),
        pltpu.VMEM((1, HD), F32),
        pltpu.VMEM((2 * D, HD), BF),
        pltpu.VMEM((D, 2 * HD), BF),
        pltpu.VMEM((D, HD), BF),
        pltpu.VMEM((NT, NY, 160, 256), BF),
        pltpu.VMEM((NT, NV, TOK, 256), BF),
        pltpu.VMEM((TOK, D), BF),
        pltpu.VMEM((NT, NC, TOK, HD), BF),
        pltpu.VMEM((NT, NC, 32, HD), BF),
        pltpu.VMEM((8, 16, VHD), BF),
        pltpu.VMEM((NT, NX, 16, VHD), BF),
        pltpu.VMEM((NT, VHD, VD), BF),
        pltpu.VMEM((8, 16, VD), BF),
        pltpu.VMEM((NX, 16, VD), BF),
        pltpu.VMEM((NV, 16, 640), BF),
        pltpu.VMEM((NV, 16, 640), BF),
        pltpu.VMEM((NV, 16, 640), BF),
        pltpu.VMEM((NX, NT, 16, 256), F32),
        pltpu.VMEM((NX, NT, 16, 256), F32),
        pltpu.VMEM((NV, NT, 16, 256), BF),
        pltpu.VMEM((32, D), BF),
        pltpu.VMEM((16, D), BF),
        pltpu.VMEM((NC, 1, 256), F32),
        pltpu.VMEM((NC, 1, 256), F32),
        pltpu.VMEM((4, 1, 1024), F32),
        dma((19,)),
        dma((8,)), dma((8,)),
        dma, dma,
        dma((NX,)), dma((NX,)),
        dma((NY,)), dma((NY,)),
        dma((NV,)), dma((NV,)),
        dma((NV,)), dma((NV,)),
        dma((NV,)), dma((NV,)),
        dma((NX,)), dma((NX,)),
        dma((NV,)), dma((NV,)),
        dma((NC,)), dma((NC,)),
        dma((NC,)), dma((NC,)),
        dma((NC,)), dma((NC,)),
        dma((5,)), dma((5,)),
        dma((NV,)), dma((NV,)),
    ]
    result = pl.pallas_call(
        kernel,
        name="fused",
        out_shape=jax.ShapeDtypeStruct((TOK, 256), BF),
        in_specs=[pl.BlockSpec(memory_space=pl.ANY)] * len(args),
        out_specs=vm,
        scratch_shapes=scratch,
        compiler_params=pltpu.CompilerParams(
            collective_id=0, has_side_effects=True, vmem_limit_bytes=63 << 20
        ),
    )(*args)
    return result.reshape(TOK, 1, 256)


def solution(mesh):
    placed = (
        P("ctx", None),
        P(),
        P(),
        P(None, None, ("vis", "tp"), None),
        P(("vis", "tp"), None, None),
        P(),
        P(),
        P("ctx", ("vis", "tp")),
        P(),
        P("ctx"),
        P(),
        P(),
        P(),
        P("ctx", ("vis", "tp")),
        P(),
        P(None, "vis", "tp", None),
        P("tp", None, "vis", None),
    )
    return jax.shard_map(
        local, mesh=mesh, in_specs=placed, out_specs=P("ctx", "vis", "tp"), check_vma=False
    )
```
